32 devices in a mesh: lat: 4 (over x, core), lon: 8 (over z, y).
Axes of the slice: x: 2, y: 2, z: 4, core: 2. Of those that a mesh axis runs over, the one named last changes fastest.
Arguments:
- tracers: float32 [4, 32, 128, 1024], P(None, None, 'lat', 'lon'), may hold values from -6 to 6
- vel_east: float32 [32, 128, 1024], P(None, 'lat', 'lon'), may hold values from -0.18 to 0.18
- vel_north: float32 [32, 128, 1024], P(None, 'lat', 'lon'), may hold values from -0.18 to 0.18
- land_mask: int32 [32, 128, 1024], P(None, 'lat', 'lon'), may hold values 0 or 1
- step_area: float32 [128, 1024], P('lat', 'lon'), may hold values from 1.5 to 4
- float_cell: int32 [2048], P(('lat', 'lon')), may hold values from 0 to 4095
- float_owner: int32 [2048, 1], P(('lat', 'lon')), may hold values from 0 to 31; in each aligned block of 64 rows (0 to 63, 64 to 127, ...) at most 4 rows name the same one
Outputs:
- tracers_out: float32 [4, 32, 128, 1024], P(None, None, 'lat', 'lon')
- arrivals: float32 [4096, 128], P(('lat', 'lon'))
- arrival_counts: int32 [1024], P(('lat', 'lon'))
The draws below stay inside these ranges and needn't reach their ends.
Inputs may be any that keep to these rules, and one draw needn't show every extreme that they name: `float_owner`: among the 64 rows of one device no device number appears more than 4 times, and in some device's rows one appears exactly 4 times.
All inputs are finite; a program needn't handle non-finite values. No bound on the sum of `land_mask` on one device may be relied on, other than what follows from the above.
Results may differ from the reference program's by a relative error of at most 0.0003.
Values sent between devices are 32-bit elements; how exact they have to be, the bound alone decides.
A program may use at most 128 MiB of HBM per device.

```python
import math
import jax
import jax.numpy as jnp
import numpy as np
from jax import lax

TRACERS = 4
LEV = 32
CLAT = 32
CLON = 128
CAP = 4
FLT_DEV = 64
FLOATS = 2048
RECW = 128
NLAT = 128
NLON = 1024
N_LON = 8
DEVICES = 32


def draw_tracers(key, part):
    base_key = jax.random.fold_in(key, 11)
    key_body, key_sign, key_size = jax.random.split(base_key, 3)
    grid_shape = (TRACERS, LEV, NLAT, NLON)
    row_local = jnp.arange(NLAT, dtype=jnp.int32) % CLAT
    col_local = jnp.arange(NLON, dtype=jnp.int32) % CLON
    row_edge = (row_local == 2) | (row_local == 3) | (row_local == CLAT - 3) | (row_local == CLAT - 4)
    col_edge = (col_local == 2) | (col_local == 3) | (col_local == CLON - 3) | (col_local == CLON - 4)
    near_edge = row_edge[:, None] | col_edge[None, :]
    flip_sign = jnp.where(jax.random.bernoulli(key_sign, 0.5, grid_shape), 1.0, -1.0).astype(jnp.float32)
    inner_values = jnp.clip(jax.random.normal(key_body, grid_shape, jnp.float32), -4.0, 4.0)
    edge_size = jax.random.uniform(key_size, grid_shape, jnp.float32, 4.0, 6.0)
    return jnp.where(near_edge[None, None], flip_sign * edge_size, inner_values).astype(jnp.float32)


def flow_field(key, salt, along_rows):
    base_key = jax.random.fold_in(key, salt)
    key_sign, key_size = jax.random.split(base_key, 2)
    grid_shape = (LEV, NLAT, NLON)
    if along_rows:
        sign_shape = (LEV, NLAT, 1)
    else:
        sign_shape = (LEV, 1, NLON)
    flip_sign = jnp.where(jax.random.bernoulli(key_sign, 0.5, sign_shape), 1.0, -1.0).astype(jnp.float32)
    magnitude = jax.random.uniform(key_size, grid_shape, jnp.float32, 0.12, 0.18)
    return (flip_sign * magnitude).astype(jnp.float32)


def draw_vel_east(key, part):
    return flow_field(key, 23, True)


def draw_vel_north(key, part):
    return flow_field(key, 37, False)


def set_ends(drawn, key, smallest, largest):
    index_at = [jax.random.randint(jax.random.fold_in(key, axis), (), 0, length) for axis, length in enumerate(drawn.shape)]
    main_axis = drawn.shape.index(max(drawn.shape))
    beside = index_at[:main_axis] + [(index_at[main_axis] + 1) % drawn.shape[main_axis]] + index_at[main_axis + 1:]
    return drawn.at[tuple(index_at)].set(smallest).at[tuple(beside)].set(largest)


def shard_levels(rng, dims, cuts, smallest, high):
    factor_of = 1.0
    for axis_at, shards_of in cuts:
        heights = jax.random.uniform(jax.random.fold_in(jax.random.fold_in(rng, 6), axis_at), (shards_of,), jnp.float32, smallest / len(cuts), high / len(cuts))
        factor_of = factor_of * jnp.repeat(jnp.exp(heights), dims[axis_at] // shards_of).reshape((-1,) + (1,) * (len(dims) - 1 - axis_at))
    return factor_of


def assign_block(own_key, own, number, rows, number_of, top, bound, skew):
    order = jax.random.permutation(own_key, number_of)
    heavy_load, ordinary = load_shares(number_of, rows * top, bound, skew, True), load_shares(number_of, rows * top, bound, skew, False)
    places = jnp.arange(number_of)

    def named(tallies, offset_by):
        used = int((tallies > 0).sum())
        fixed = max(1, used // 4)
        passed = fixed + (places - fixed + offset_by * (used - fixed)) % max(1, number_of - fixed)
        return jnp.zeros((number_of,), jnp.int32).at[order[jnp.where(places < fixed, places, passed)]].set(jnp.asarray(tallies, jnp.int32))

    tallies = jnp.where(number % 4 == 0, named(heavy_load, number // 4), named(ordinary, number - number // 4 - 1))
    mixed = jax.random.permutation(jax.random.fold_in(own, 3), number_of)
    giver, receiver = mixed[0:number_of // 2 * 2:2], mixed[1:number_of // 2 * 2:2]
    slack = jnp.minimum(tallies[giver] - 1, bound - tallies[receiver]) // 2
    slack = jnp.where((giver == order[0]) | (receiver == order[0]) | (tallies[receiver] == 0), 0, jnp.maximum(slack, 0))
    passed = jax.random.randint(jax.random.fold_in(own, 4), (number_of // 2,), 0, 1 << 20) % (slack + 1)
    tallies = tallies.at[giver].add(-passed).at[receiver].add(passed)
    items = jnp.searchsorted(jnp.cumsum(tallies), jnp.arange(rows * top), side="right").astype(jnp.int32)
    listing = items.reshape(top, rows).T
    listing = listing[jax.random.permutation(jax.random.fold_in(own, 1), rows)]
    offset_by = jax.random.randint(jax.random.fold_in(own, 2), (rows, 1), 0, top)
    return jnp.take_along_axis(listing, (jnp.arange(top)[None, :] + offset_by) % top, axis=1)


def load_shares(amount, total, most, skew, full):
    loads = [(1 << 20) // math.isqrt(rank ** skew) + 1 for rank in range(1, amount + 1)]
    largest = most if full else min(most, max(-(-total // amount), total * loads[0] // sum(loads)))
    least = 1 if total - largest >= amount - 1 else 0
    holding, rest = [largest] + [least] * (amount - 1), total - largest - least * (amount - 1)
    while rest > 0:
        candidates = [i for i in range(1, amount) if holding[i] < largest] or [i for i in range(1, amount) if holding[i] < most]
        mass, left = sum([loads[i] for i in candidates]), rest
        for i in candidates:
            extra = min(most - holding[i], max(1, left * loads[i] // mass), rest)
            holding[i] = holding[i] + extra
            rest = rest - extra
    return np.array(holding)


def setup_inputs(seed: int = 0) -> dict:
    splits = jax.random.split(jax.random.key(seed), 8)
    tracers = draw_tracers(jax.random.fold_in(splits[7], 71), 0)
    vel_east = draw_vel_east(jax.random.fold_in(splits[7], 71), 0)
    vel_north = draw_vel_north(jax.random.fold_in(splits[7], 71), 0)
    land_mask = set_ends((jax.random.randint(splits[3], (LEV, NLAT, NLON), 0, 8) < 7).astype(jnp.int32), jax.random.fold_in(splits[3], 1), 0, 1)
    step_area = jnp.clip(jnp.exp(math.log(4.0) - 0.98082925 * jax.random.uniform(splits[4], (NLAT, NLON), jnp.float32) ** shard_levels(splits[4], (NLAT, NLON), ((0, 4), (1, 8)), -0.2, 0.2)), 1.5, 4.0)
    float_cell = set_ends(jax.random.randint(splits[5], (FLOATS,), 0, CLAT * CLON), jax.random.fold_in(splits[5], 1), 0, (CLAT * CLON) - 1).astype(jnp.int32)
    float_owner_keys = jax.random.split(jax.random.fold_in(splits[6], 1), FLOATS // FLT_DEV)
    float_owner_turns = jax.random.permutation(jax.random.fold_in(splits[6], 3), FLOATS // FLT_DEV)
    float_owner = jax.vmap(lambda own, number: assign_block(jax.random.fold_in(splits[6], 2), own, number, FLT_DEV, DEVICES, 1, CAP, 2))(float_owner_keys, float_owner_turns).reshape((FLOATS, 1))
    return {"tracers": tracers, "vel_east": vel_east, "vel_north": vel_north, "land_mask": land_mask, "step_area": step_area, "float_cell": float_cell, "float_owner": float_owner}


def face_flux(velocity, behind, current, forward, farther):
    return velocity * (7.0 * (current + forward) - (behind + farther)) / 12.0 - jnp.abs(velocity) * (3.0 * (forward - current) - (farther - behind)) / 12.0


def advance(tracer_pad, static_pad, step_area, row_count, col_count):
    flow_east, flow_north, wet_pad = static_pad[0], static_pad[1], static_pad[2]
    lon_strip = tracer_pad[..., 2:row_count + 2, :]
    open_east = flow_east[:, 2:row_count + 2, 1:col_count + 2] * wet_pad[:, 2:row_count + 2, 1:col_count + 2] * wet_pad[:, 2:row_count + 2, 2:col_count + 3]
    flux_x = face_flux(open_east, lon_strip[..., 0:col_count + 1], lon_strip[..., 1:col_count + 2], lon_strip[..., 2:col_count + 3], lon_strip[..., 3:col_count + 4])
    lat_strip = tracer_pad[..., 2:col_count + 2]
    open_north = flow_north[:, 1:row_count + 2, 2:col_count + 2] * wet_pad[:, 1:row_count + 2, 2:col_count + 2] * wet_pad[:, 2:row_count + 3, 2:col_count + 2]
    flux_y = face_flux(open_north, lat_strip[..., 0:row_count + 1, :], lat_strip[..., 1:row_count + 2, :], lat_strip[..., 2:row_count + 3, :], lat_strip[..., 3:row_count + 4, :])
    change = (flux_x[..., 1:] - flux_x[..., :-1]) + (flux_y[..., 1:, :] - flux_y[..., :-1, :])
    centre = tracer_pad[..., 2:row_count + 2, 2:col_count + 2]
    return centre - step_area * wet_pad[:, 2:row_count + 2, 2:col_count + 2] * change


def extend(field_in, folded):
    fold_rows = jnp.flip(field_in[..., NLAT - 2:, :], axis=(-2, -1))
    if not folded:
        fold_rows = jnp.zeros_like(fold_rows)
    low_rows = jnp.zeros_like(field_in[..., :2, :])
    lat_padded = jnp.concatenate([low_rows, field_in, fold_rows], axis=-2)
    return jnp.concatenate([lat_padded[..., -2:], lat_padded, lat_padded[..., :2]], axis=-1)


def reference(tracers, vel_east, vel_north, land_mask, step_area, float_cell, float_owner):
    wet_mask = land_mask.astype(jnp.float32)
    static_pad = jnp.stack([extend(vel_east, False), extend(vel_north, False), extend(wet_mask, True)])

    def advect_one(single):
        after_one = advance(extend(single, True), static_pad, step_area, NLAT, NLON)
        return advance(extend(after_one, True), static_pad, step_area, NLAT, NLON)

    finished = lax.map(advect_one, tracers)
    row_index = jnp.arange(FLOATS, dtype=jnp.int32)
    source = row_index // FLT_DEV
    band_index = source // N_LON
    slab_index = source % N_LON
    grid_lat = band_index * CLAT + float_cell // CLON
    grid_lon = slab_index * CLON + float_cell % CLON
    samples = finished[:, :, grid_lat, grid_lon]
    records = jnp.transpose(samples, (2, 0, 1)).reshape(FLOATS, RECW)
    owner = float_owner[:, 0]
    blocks = owner.reshape(DEVICES, FLT_DEV)
    local_index = jnp.arange(FLT_DEV, dtype=jnp.int32)
    earlier = local_index[None, :] < local_index[:, None]
    same_owner = (blocks[:, :, None] == blocks[:, None, :]) & earlier[None]
    slot_rank = jnp.sum(same_owner.astype(jnp.int32), axis=2).reshape(FLOATS)
    slot_index = owner * (DEVICES * CAP) + source * CAP + slot_rank
    arrivals = jnp.zeros((DEVICES * DEVICES * CAP, RECW), jnp.float32).at[slot_index].set(records)
    arrival_counts = jnp.zeros((DEVICES * DEVICES,), jnp.int32).at[owner * DEVICES + source].add(jnp.ones((FLOATS,), jnp.int32))
    return finished, arrivals, arrival_counts
```

```python
import functools

import jax
import jax.numpy as jnp
from jax import lax
from jax.experimental import pallas as pl
from jax.experimental.pallas import tpu as pltpu
from jax.sharding import PartitionSpec as P

CAP = 4
BOX = 8
PADR = 8
MESH = pl.DeviceIdType.MESH


def kernel(
    dims, area_h, cell_h, owner_h, mask_h, east_h, north_h, tracers_h, out_h, arrivals, counts,
    area, cell, owner, mask, east, north, first, second, final, wet, flow, coef,
    cols, send_l, send_r, get_l, get_r, send_n, send_s, get_n, get_s,
    pick, halves, outbox, inbox,
    in_sem, out_sem, halo_send, halo_recv, box_send, box_recv,
):
    tracer_count, levels, rows, n_lat, n_lon = dims
    planes = tracer_count * levels
    tall = rows + 2 * PADR
    n_dev = n_lat * n_lon
    slots = n_dev * BOX
    floats = cell.shape[1]
    lat, lon = lax.axis_index("lat"), lax.axis_index("lon")
    me = lat * n_lon + lon
    top = lat == n_lat - 1
    bottom = lat == 0

    loads = [
        pltpu.make_async_copy(mask_h, mask, in_sem.at[0]),
        pltpu.make_async_copy(east_h, east, in_sem.at[1]),
        pltpu.make_async_copy(north_h, north, in_sem.at[2]),
        pltpu.make_async_copy(tracers_h, first.at[:, pl.ds(PADR, rows), :], in_sem.at[3]),
        pltpu.make_async_copy(area_h, area, in_sem.at[4]),
        pltpu.make_async_copy(cell_h, cell, in_sem.at[5]),
        pltpu.make_async_copy(owner_h, owner, in_sem.at[6]),
    ]
    for load in loads:
        load.start()

    barrier = pltpu.get_barrier_semaphore()

    def greet(j, carry):
        other = lax.rem(me + j, n_dev)
        pl.semaphore_signal(
            barrier, inc=1, device_id=(other // n_lon, lax.rem(other, n_lon)), device_id_type=MESH
        )
        return carry

    lax.fori_loop(1, n_dev, greet, 0)

    lane = lax.broadcasted_iota(jnp.int32, (8, 128), 1)
    group = lane // 4
    low_pair = lax.rem(lane, 4) < 2
    lane_all = lax.broadcasted_iota(jnp.int32, (rows, 128), 1)
    low_all = lax.rem(lane_all, 4) < 2
    groups = rows // 8

    for load in loads[:4]:
        load.wait()

    def gather_columns(k, acc):
        acc = list(acc)
        here = group == k
        for g in range(groups):
            at = pl.ds(PADR + 8 * g, 8)
            sub = pl.ds(8 * g, 8)
            water = mask[k, sub, :].astype(jnp.float32)
            wet[k, at, :] = water
            flow[k, at, :] = north[k, sub, :] * water
            edge = jnp.where(lane == 0, water, east[k, sub, :] * water)
            values = [first[c * levels + k, at, :] for c in range(tracer_count)] + [edge]
            for c, value in enumerate(values):
                i = c * groups + g
                acc[i] = jnp.where(here, pltpu.roll(value, 4 * k + 2, 1), acc[i])
        return tuple(acc)

    blank = jnp.zeros((8, 128), jnp.float32)
    packed = lax.fori_loop(0, levels, gather_columns, (blank,) * ((tracer_count + 1) * groups))

    def fill_columns(packed, step):
        for pair in range(tracer_count // 2):
            for g in range(groups):
                a, b = packed[2 * pair * groups + g], packed[(2 * pair + 1) * groups + g]
                sub = pl.ds(pair * rows + 8 * g, 8)
                send_r[step, sub, :] = jnp.where(low_pair, a, pltpu.roll(b, 2, 1))
                send_l[step, sub, :] = jnp.where(low_pair, pltpu.roll(b, 126, 1), a)
        if step == 0:
            for g in range(groups):
                value = packed[tracer_count * groups + g]
                sub = pl.ds(tracer_count // 2 * rows + 8 * g, 8)
                send_r[step, sub, :] = value
                send_l[step, sub, :] = value

    def fill_rows(field, step):
        flat = field.reshape(planes * tall, 128)
        wet_flat = wet.reshape(levels * tall, 128)
        flow_flat = flow.reshape(levels * tall, 128)

        def row(r):
            return flat[pl.ds(PADR + r, planes, stride=tall), :]

        @pl.when(jnp.logical_not(top))
        def _():
            send_n[step, pl.ds(0, planes), :] = row(rows - 2)
            send_n[step, pl.ds(planes, planes), :] = row(rows - 1)
            if step == 0:
                send_n[step, pl.ds(2 * planes, levels), :] = flow_flat[
                    pl.ds(PADR + rows - 1, levels, stride=tall), :
                ]

        @pl.when(top)
        def _():
            ahead = lax.broadcasted_iota(jnp.int32, (128, 128), 0)
            across = lax.broadcasted_iota(jnp.int32, (128, 128), 1)
            turn = (ahead + across == 127).astype(jnp.float32)

            def turned(value):
                return jnp.dot(
                    value, turn, precision=lax.Precision.HIGHEST, preferred_element_type=jnp.float32
                )

            send_n[step, pl.ds(0, planes), :] = turned(row(rows - 1))
            send_n[step, pl.ds(planes, planes), :] = turned(row(rows - 2))
            if step == 0:
                send_n[step, pl.ds(2 * planes, levels), :] = turned(
                    wet_flat[pl.ds(PADR + rows - 1, levels, stride=tall), :]
                )

        send_s[step, pl.ds(0, planes), :] = row(0)
        send_s[step, pl.ds(planes, planes), :] = row(1)
        if step == 0:
            send_s[step, pl.ds(2 * planes, levels), :] = wet_flat[
                pl.ds(PADR, levels, stride=tall), :
            ]

    right, left = lax.rem(lon + 1, n_lon), lax.rem(lon + n_lon - 1, n_lon)
    upper = (jnp.where(top, lat, lat + 1), jnp.where(top, n_lon - 1 - lon, lon))
    lower = (jnp.where(bottom, 0, lat - 1), lon)

    def halo_copies(step):
        row_size = 2 * planes + (levels if step == 0 else 0)
        col_size = tracer_count // 2 * rows + (rows if step == 0 else 0)
        plan = (
            (send_r, get_l, col_size, (lat, right)),
            (send_l, get_r, col_size, (lat, left)),
            (send_n, get_s, row_size, upper),
            (send_s, get_n, row_size, lower),
        )
        return [
            pltpu.make_async_remote_copy(
                src_ref=source.at[step, pl.ds(0, size)],
                dst_ref=target.at[step, pl.ds(0, size)],
                send_sem=halo_send.at[step, i],
                recv_sem=halo_recv.at[step, i],
                device_id=device,
                device_id_type=MESH,
            )
            for i, (source, target, size, device) in enumerate(plan)
        ]

    def start_halos(step):
        east_copy, west_copy, up_copy, down_copy = halo_copies(step)
        row_size = 2 * planes + (levels if step == 0 else 0)
        fold_copy = pltpu.make_async_remote_copy(
            src_ref=send_n.at[step, pl.ds(0, row_size)],
            dst_ref=get_n.at[step, pl.ds(0, row_size)],
            send_sem=halo_send.at[step, 2],
            recv_sem=halo_recv.at[step, 3],
            device_id=upper,
            device_id_type=MESH,
        )

        @pl.when(jnp.logical_not(top))
        def _():
            up_copy.start()

        @pl.when(top)
        def _():
            fold_copy.start()

        @pl.when(jnp.logical_not(bottom))
        def _():
            down_copy.start()

        east_copy.start()
        west_copy.start()

    def wait_halos(step):
        east_copy, west_copy, up_copy, down_copy = halo_copies(step)
        east_copy.wait()
        west_copy.wait()
        up_copy.wait_send()
        down_copy.wait_recv()

        @pl.when(jnp.logical_not(bottom))
        def _():
            down_copy.wait_send()
            up_copy.wait_recv()

    def place_halos(field, step):
        flat = field.reshape(planes * tall, 128)
        wet_flat = wet.reshape(levels * tall, 128)
        flow_flat = flow.reshape(levels * tall, 128)
        for i in range(2):
            flat[pl.ds(PADR + rows + i, planes, stride=tall), :] = get_n[
                step, pl.ds(i * planes, planes), :
            ]
        if step == 0:
            wet_flat[pl.ds(PADR + rows, levels, stride=tall), :] = get_n[
                step, pl.ds(2 * planes, levels), :
            ]

        @pl.when(bottom)
        def _():
            for i in range(2):
                flat[pl.ds(PADR - 2 + i, planes, stride=tall), :] = jnp.zeros((planes, 128), jnp.float32)
            if step == 0:
                flow_flat[pl.ds(PADR - 1, levels, stride=tall), :] = jnp.zeros((levels, 128), jnp.float32)

        @pl.when(jnp.logical_not(bottom))
        def _():
            for i in range(2):
                flat[pl.ds(PADR - 2 + i, planes, stride=tall), :] = get_s[
                    step, pl.ds(i * planes, planes), :
                ]
            if step == 0:
                flow_flat[pl.ds(PADR - 1, levels, stride=tall), :] = get_s[
                    step, pl.ds(2 * planes, levels), :
                ]

        for pair in range(tracer_count // 2):
            from_l = get_l[step, pl.ds(pair * rows, rows), :]
            from_r = get_r[step, pl.ds(pair * rows, rows), :]
            cols[2 * pair] = jnp.where(low_all, from_l, from_r)
            cols[2 * pair + 1] = jnp.where(
                low_all, pltpu.roll(from_l, 126, 1), pltpu.roll(from_r, 2, 1)
            )
        if step == 0:
            sub = pl.ds(tracer_count // 2 * rows, rows)
            cols[tracer_count] = jnp.where(low_all, get_l[step, sub, :], get_r[step, sub, :])

    def make_coefficients(k, g):
        at = pl.ds(PADR + 8 * g, 8)
        sub = pl.ds(8 * g, 8)
        beside = pltpu.roll(cols[tracer_count, sub, :], 126 - 4 * k, 1)
        water = wet[k, at, :]
        scale = area[sub, :] * water * (1.0 / 6.0)
        stream = east[k, sub, :] * water
        face_e = stream * pltpu.roll(jnp.where(lane == 0, beside, water), 127, 1)
        face_w = pltpu.roll(jnp.where(lane == 127, beside, stream), 1, 1) * water
        face_n = flow[k, at, :] * wet[k, pl.ds(PADR + 8 * g + 1, 8), :]
        face_s = flow[k, pl.ds(PADR + 8 * g - 1, 8), :] * water
        made = []
        centre = 1.0
        for ahead, behind in ((face_e, face_w), (face_n, face_s)):
            pos, neg = jnp.maximum(ahead, 0.0) * scale, jnp.minimum(ahead, 0.0) * scale
            pos_b, neg_b = jnp.maximum(behind, 0.0) * scale, jnp.minimum(behind, 0.0) * scale
            centre = centre - (5.0 * (pos - neg_b) + 2.0 * (neg - pos_b))
            made += [
                -pos_b,
                pos + 5.0 * pos_b + 2.0 * neg_b,
                -(2.0 * pos + 5.0 * neg + neg_b),
                neg,
            ]
        return [centre] + made

    def apply(field, k, g, c, weights):
        centre, xm2, xm1, xp1, xp2, ym2, ym1, yp1, yp2 = weights
        plane = c * levels + k
        base = PADR + 8 * g
        value = field[plane, pl.ds(base, 8), :]
        beside = pltpu.roll(cols[c, pl.ds(8 * g, 8), :], 126 - 4 * k, 1)
        total = centre * value
        total += xm2 * pltpu.roll(jnp.where(lane >= 126, beside, value), 2, 1)
        total += xm1 * pltpu.roll(jnp.where(lane == 127, beside, value), 1, 1)
        total += xp1 * pltpu.roll(jnp.where(lane == 0, beside, value), 127, 1)
        total += xp2 * pltpu.roll(jnp.where(lane <= 1, beside, value), 126, 1)
        total += ym2 * field[plane, pl.ds(base - 2, 8), :]
        total += ym1 * field[plane, pl.ds(base - 1, 8), :]
        total += yp1 * field[plane, pl.ds(base + 1, 8), :]
        total += yp2 * field[plane, pl.ds(base + 2, 8), :]
        return total

    def first_step(k, acc):
        acc = list(acc)
        here = group == k
        for g in range(groups):
            weights = make_coefficients(k, g)
            for n, weight in enumerate(weights):
                coef[k, n, pl.ds(8 * g, 8), :] = weight
            for c in range(tracer_count):
                value = apply(first, k, g, c, weights)
                second[c * levels + k, pl.ds(PADR + 8 * g, 8), :] = value
                i = c * groups + g
                acc[i] = jnp.where(here, pltpu.roll(value, 4 * k + 2, 1), acc[i])
        return tuple(acc)

    def second_step(k, carry):
        for g in range(groups):
            weights = [coef[k, n, pl.ds(8 * g, 8), :] for n in range(9)]
            for c in range(tracer_count):
                final[c * levels + k, pl.ds(8 * g, 8), :] = apply(second, k, g, c, weights)
        return carry

    fill_columns(packed, 0)
    fill_rows(first, 0)
    pl.semaphore_wait(barrier, n_dev - 1)
    start_halos(0)

    for load in loads[4:]:
        load.wait()
    cell_row, owner_row = cell[...], owner[...]
    f_row = lax.broadcasted_iota(jnp.int32, (floats, floats), 0)
    f_col = lax.broadcasted_iota(jnp.int32, (floats, floats), 1)
    diagonal = f_row == f_col
    owner_f = owner_row.astype(jnp.float32)
    owner_col = jnp.sum(jnp.where(diagonal, owner_f, 0.0), axis=1, keepdims=True)
    cell_col = jnp.sum(jnp.where(diagonal, cell_row.astype(jnp.float32), 0.0), axis=1, keepdims=True)
    rank = jnp.sum(
        jnp.where((owner_col == owner_f) & (f_col < f_row), 1.0, 0.0), axis=1, keepdims=True
    )
    slot_col = owner_col * float(BOX) + rank
    slot_lane = lax.broadcasted_iota(jnp.int32, (floats, slots), 1).astype(jnp.float32)
    wanted = jnp.sum(jnp.where(slot_col == slot_lane, cell_col + 1.0, 0.0), axis=0, keepdims=True) - 1.0
    wanted = wanted.astype(jnp.int32)
    slot_row = lax.broadcasted_iota(jnp.int32, (slots, floats), 0)
    tally = jnp.sum(
        jnp.where(owner_row * BOX + CAP == slot_row, 1.0, 0.0), axis=1, keepdims=True
    )

    def mark(r, carry):
        start = pl.multiple_of(r * 128, 128)
        place = lax.broadcasted_iota(jnp.int32, (128, slots), 0) + start
        pick[pl.ds(start, 128), :] = jnp.where(place == wanted, 1.0, 0.0).astype(jnp.bfloat16)
        return carry

    lax.fori_loop(0, rows, mark, 0)

    wait_halos(0)
    place_halos(first, 0)
    packed = lax.fori_loop(0, levels, first_step, (blank,) * (tracer_count * groups))
    fill_columns(packed, 1)
    fill_rows(second, 1)
    start_halos(1)
    wait_halos(1)
    place_halos(second, 1)
    lax.fori_loop(0, levels, second_step, 0)
    store = pltpu.make_async_copy(final, out_h, out_sem.at[0])
    store.start()

    flat = final.reshape(planes * rows, 128)
    for r in range(rows):
        value = flat[pl.ds(r, planes, stride=rows), :]
        high = value.astype(jnp.bfloat16)
        rest = (value - high.astype(jnp.float32)).astype(jnp.bfloat16)
        halves[pl.ds(0, planes), pl.ds(r * 128, 128)] = high
        halves[pl.ds(planes, planes), pl.ds(r * 128, 128)] = rest
    taken = jnp.dot(halves[...], pick[...], preferred_element_type=jnp.float32)
    outbox[...] = jnp.transpose(taken[:planes] + taken[planes:]) + tally

    def box_copy(j):
        other = lax.rem(me + j, n_dev)
        return pltpu.make_async_remote_copy(
            src_ref=outbox.at[pl.ds(pl.multiple_of(other * BOX, BOX), BOX)],
            dst_ref=inbox.at[pl.ds(pl.multiple_of(me * BOX, BOX), BOX)],
            send_sem=box_send.at[other],
            recv_sem=box_recv.at[me],
            device_id=(other // n_lon, lax.rem(other, n_lon)),
            device_id_type=MESH,
        )

    def box_start(j, carry):
        box_copy(j).start()
        return carry

    def box_wait(j, carry):
        other = lax.rem(me + j, n_dev)
        at = pl.ds(pl.multiple_of(other * BOX, BOX), BOX)
        copy = pltpu.make_async_remote_copy(
            src_ref=outbox.at[at],
            dst_ref=inbox.at[at],
            send_sem=box_send.at[other],
            recv_sem=box_recv.at[other],
            device_id=(other // n_lon, lax.rem(other, n_lon)),
            device_id_type=MESH,
        )
        copy.wait()
        return carry

    lax.fori_loop(1, n_dev, box_start, 0)
    own = pl.ds(pl.multiple_of(me * BOX, BOX), BOX)
    inbox[own, :] = outbox[own, :]
    lax.fori_loop(1, n_dev, box_wait, 0)
    for i in range(CAP):
        arrivals[pl.ds(i, n_dev, stride=CAP), :] = inbox[pl.ds(i, n_dev, stride=BOX), :]
    told = inbox[pl.ds(CAP, n_dev, stride=BOX), :][:, :n_dev]
    straight = lax.broadcasted_iota(jnp.int32, (n_dev, n_dev), 0) == lax.broadcasted_iota(
        jnp.int32, (n_dev, n_dev), 1
    )
    counts[...] = jnp.sum(jnp.where(straight, told, 0.0), axis=0, keepdims=True).astype(jnp.int32)
    store.wait()


def local(tracers, vel_east, vel_north, land_mask, step_area, float_cell, float_owner):
    tracer_count, levels, rows, columns = tracers.shape
    n_lat, n_lon = lax.axis_size("lat"), lax.axis_size("lon")
    n_dev = n_lat * n_lon
    planes = tracer_count * levels
    tall = rows + 2 * PADR
    floats = float_cell.shape[0]
    row_size = 2 * planes + levels
    col_size = (tracer_count // 2 + 1) * rows
    f32 = jnp.float32
    whole = pl.BlockSpec(memory_space=pl.ANY)
    vmem = pl.BlockSpec(memory_space=pltpu.VMEM)
    out, arrivals, counts = pl.pallas_call(
        functools.partial(kernel, (tracer_count, levels, rows, n_lat, n_lon)),
        out_shape=(
            jax.ShapeDtypeStruct((planes, rows, columns), f32),
            jax.ShapeDtypeStruct((n_dev * CAP, planes), f32),
            jax.ShapeDtypeStruct((1, n_dev), jnp.int32),
        ),
        in_specs=[whole] * 7,
        out_specs=(whole, vmem, vmem),
        scratch_shapes=[
            pltpu.VMEM((rows, columns), f32),
            pltpu.VMEM((1, floats), jnp.int32),
            pltpu.VMEM((1, floats), jnp.int32),
            pltpu.VMEM((levels, rows, columns), jnp.int32),
            pltpu.VMEM((levels, rows, columns), f32),
            pltpu.VMEM((levels, rows, columns), f32),
            pltpu.VMEM((planes, tall, columns), f32),
            pltpu.VMEM((planes, tall, columns), f32),
            pltpu.VMEM((planes, rows, columns), f32),
            pltpu.VMEM((levels, tall, columns), f32),
            pltpu.VMEM((levels, tall, columns), f32),
            pltpu.VMEM((levels, 9, rows, columns), f32),
            pltpu.VMEM((tracer_count + 1, rows, columns), f32),
            *[pltpu.VMEM((2, col_size, columns), f32)] * 4,
            *[pltpu.VMEM((2, row_size, columns), f32)] * 4,
            pltpu.VMEM((rows * columns, n_dev * BOX), jnp.bfloat16),
            pltpu.VMEM((2 * planes, rows * columns), jnp.bfloat16),
            pltpu.VMEM((n_dev * BOX, planes), f32),
            pltpu.VMEM((n_dev * BOX, planes), f32),
            pltpu.SemaphoreType.DMA((7,)),
            pltpu.SemaphoreType.DMA((1,)),
            pltpu.SemaphoreType.DMA((2, 4)),
            pltpu.SemaphoreType.DMA((2, 4)),
            pltpu.SemaphoreType.DMA((n_dev,)),
            pltpu.SemaphoreType.DMA((n_dev,)),
        ],
        compiler_params=pltpu.CompilerParams(
            collective_id=0, has_side_effects=True, vmem_limit_bytes=56 * 1024 * 1024
        ),
        cost_estimate=pl.CostEstimate(
            flops=2 * 17 * planes * rows * columns, bytes_accessed=8 * 1024 * 1024, transcendentals=0
        ),
    )(
        step_area,
        float_cell.reshape(1, floats),
        float_owner.reshape(1, floats),
        land_mask,
        vel_east,
        vel_north,
        tracers.reshape(planes, rows, columns),
    )
    return out.reshape(tracers.shape), arrivals, counts.reshape(n_dev)


def solution(mesh):
    placed = (
        P(None, None, "lat", "lon"),
        P(None, "lat", "lon"),
        P(None, "lat", "lon"),
        P(None, "lat", "lon"),
        P("lat", "lon"),
        P(("lat", "lon")),
        P(("lat", "lon"), None),
    )
    return jax.shard_map(
        local,
        mesh=mesh,
        in_specs=placed,
        out_specs=(P(None, None, "lat", "lon"), P(("lat", "lon"), None), P(("lat", "lon"))),
        check_vma=False,
    )
```

```python
import functools

import jax
import jax.numpy as jnp
from jax import lax
from jax.experimental import pallas as pl
from jax.experimental.pallas import tpu as pltpu
from jax.sharding import PartitionSpec as P

CAP = 4
BOX = 8
PADR = 8
MESH = pl.DeviceIdType.MESH


def kernel(
    dims, area_h, cell_h, owner_h, mask_h, east_h, north_h, tracers_h, final, arrivals, counts,
    area, cell, owner, mask, east, north, first, second, wet, flow, coef,
    cols, send_l, send_r, get_l, get_r, send_n, send_s, get_n, get_s,
    pick, halves, taken, outbox, inbox,
    in_sem, halo_send, halo_recv, box_send, box_recv,
):
    tracer_count, levels, rows, n_lat, n_lon = dims
    planes = tracer_count * levels
    tall = rows + 2 * PADR
    n_dev = n_lat * n_lon
    slots = n_dev * BOX
    floats = cell.shape[1]
    lat, lon = lax.axis_index("lat"), lax.axis_index("lon")
    me = lat * n_lon + lon
    top = lat == n_lat - 1
    bottom = lat == 0

    loads = [
        pltpu.make_async_copy(mask_h, mask, in_sem.at[0]),
        pltpu.make_async_copy(east_h, east, in_sem.at[1]),
        pltpu.make_async_copy(north_h, north, in_sem.at[2]),
        pltpu.make_async_copy(tracers_h, first.at[:, pl.ds(PADR, rows), :], in_sem.at[3]),
        pltpu.make_async_copy(area_h, area, in_sem.at[4]),
        pltpu.make_async_copy(cell_h, cell, in_sem.at[5]),
        pltpu.make_async_copy(owner_h, owner, in_sem.at[6]),
    ]
    for load in loads:
        load.start()

    barrier = pltpu.get_barrier_semaphore()

    def greet(j, carry):
        other = lax.rem(me + j, n_dev)
        pl.semaphore_signal(
            barrier, inc=1, device_id=(other // n_lon, lax.rem(other, n_lon)), device_id_type=MESH
        )
        return carry

    lax.fori_loop(1, n_dev, greet, 0)

    lane = lax.broadcasted_iota(jnp.int32, (8, 128), 1)
    group = lane // 4
    low_pair = lax.rem(lane, 4) < 2
    groups = rows // 8

    inner, outer = tuple(range(1, groups - 1)), (0, groups - 1)
    parts = (inner, outer)
    pairs = tracer_count // 2
    first_flat = first.reshape(planes * tall, 128)
    second_flat = second.reshape(planes * tall, 128)
    wet_flat = wet.reshape(levels * tall, 128)
    flow_flat = flow.reshape(levels * tall, 128)
    blank = jnp.zeros((8, 128), jnp.float32)

    for load in loads[:4]:
        load.wait()

    def gather_columns(k, acc):
        acc = list(acc)
        here = group == k
        for g in range(groups):
            at = pl.ds(PADR + 8 * g, 8)
            sub = pl.ds(8 * g, 8)
            water = mask[k, sub, :].astype(jnp.float32)
            wet[k, at, :] = water
            flow[k, at, :] = north[k, sub, :] * water
            edge = jnp.where(lane == 0, water, east[k, sub, :] * water)
            values = [first[c * levels + k, at, :] for c in range(tracer_count)] + [edge]
            for c, value in enumerate(values):
                i = g * (tracer_count + 1) + c
                acc[i] = jnp.where(here, pltpu.roll(value, 4 * k + 2, 1), acc[i])
        return tuple(acc)

    def fill_columns(packed, step, part):
        per = len(packed) // len(parts[part])
        for n in range(len(parts[part])):
            mine = packed[n * per : (n + 1) * per]
            for pair in range(pairs):
                a, b = mine[2 * pair], mine[2 * pair + 1]
                sub = pl.ds(pair * 8 * len(parts[part]) + 8 * n, 8)
                send_r[step, part, sub, :] = jnp.where(low_pair, a, pltpu.roll(b, 2, 1))
                send_l[step, part, sub, :] = jnp.where(low_pair, pltpu.roll(b, 126, 1), a)
            if step == 0:
                sub = pl.ds(pairs * 8 * len(parts[part]) + 8 * n, 8)
                send_r[step, part, sub, :] = mine[tracer_count]
                send_l[step, part, sub, :] = mine[tracer_count]

    def place_columns(step, part):
        for n, g in enumerate(parts[part]):
            at = pl.ds(8 * g, 8)
            for pair in range(pairs):
                sub = pl.ds(pair * 8 * len(parts[part]) + 8 * n, 8)
                from_l, from_r = get_l[step, part, sub, :], get_r[step, part, sub, :]
                cols[2 * pair, at, :] = jnp.where(low_pair, from_l, from_r)
                cols[2 * pair + 1, at, :] = jnp.where(
                    low_pair, pltpu.roll(from_l, 126, 1), pltpu.roll(from_r, 2, 1)
                )
            if step == 0:
                sub = pl.ds(pairs * 8 * len(parts[part]) + 8 * n, 8)
                cols[tracer_count, at, :] = jnp.where(
                    low_pair, get_l[step, part, sub, :], get_r[step, part, sub, :]
                )

    def fill_rows(flat, step):
        def row(r):
            return flat[pl.ds(PADR + r, planes, stride=tall), :]

        def water(r):
            line = mask.reshape(levels * rows, 128)[pl.ds(r, levels, stride=rows), :]
            return line.astype(jnp.float32)

        def stream(r):
            return north.reshape(levels * rows, 128)[pl.ds(r, levels, stride=rows), :] * water(r)

        @pl.when(jnp.logical_not(top))
        def _():
            send_n[step, pl.ds(0, planes), :] = row(rows - 2)
            send_n[step, pl.ds(planes, planes), :] = row(rows - 1)
            if step == 0:
                send_n[step, pl.ds(2 * planes, levels), :] = stream(rows - 1)

        @pl.when(top)
        def _():
            ahead = lax.broadcasted_iota(jnp.int32, (128, 128), 0)
            across = lax.broadcasted_iota(jnp.int32, (128, 128), 1)
            turn = (ahead + across == 127).astype(jnp.float32)

            def turned(value):
                return jnp.dot(
                    value, turn, precision=lax.Precision.HIGHEST, preferred_element_type=jnp.float32
                )

            send_n[step, pl.ds(0, planes), :] = turned(row(rows - 1))
            send_n[step, pl.ds(planes, planes), :] = turned(row(rows - 2))
            if step == 0:
                send_n[step, pl.ds(2 * planes, levels), :] = turned(water(rows - 1))

        send_s[step, pl.ds(0, planes), :] = row(0)
        send_s[step, pl.ds(planes, planes), :] = row(1)
        if step == 0:
            send_s[step, pl.ds(2 * planes, levels), :] = water(0)

    right, left = lax.rem(lon + 1, n_lon), lax.rem(lon + n_lon - 1, n_lon)
    upper = (jnp.where(top, lat, lat + 1), jnp.where(top, n_lon - 1 - lon, lon))
    lower = (jnp.where(bottom, 0, lat - 1), lon)

    def column_copies(step, part):
        size = (pairs + (1 if step == 0 else 0)) * 8 * len(parts[part])
        return [
            pltpu.make_async_remote_copy(
                src_ref=source.at[step, part, pl.ds(0, size)],
                dst_ref=target.at[step, part, pl.ds(0, size)],
                send_sem=halo_send.at[step, 2 * part + i],
                recv_sem=halo_recv.at[step, 2 * part + i],
                device_id=(lat, device),
                device_id_type=MESH,
            )
            for i, (source, target, device) in enumerate(
                ((send_r, get_l, right), (send_l, get_r, left))
            )
        ]

    def start_columns(step, part):
        for copy in column_copies(step, part):
            copy.start()

    def wait_columns(step, part):
        for copy in column_copies(step, part):
            copy.wait()

    def row_copy(step, source, target, out, come, device):
        size = 2 * planes + (levels if step == 0 else 0)
        return pltpu.make_async_remote_copy(
            src_ref=source.at[step, pl.ds(0, size)],
            dst_ref=target.at[step, pl.ds(0, size)],
            send_sem=halo_send.at[step, out],
            recv_sem=halo_recv.at[step, come],
            device_id=device,
            device_id_type=MESH,
        )

    def up_copy(step):
        return row_copy(step, send_n, get_s, 4, 4, upper)

    def down_copy(step):
        return row_copy(step, send_s, get_n, 5, 5, lower)

    def fold_copy(step):
        return row_copy(step, send_n, get_n, 4, 5, upper)

    def start_rows(step):
        @pl.when(top)
        def _():
            fold_copy(step).start()

        @pl.when(jnp.logical_not(top))
        def _():
            up_copy(step).start()

        @pl.when(jnp.logical_not(bottom))
        def _():
            down_copy(step).start()

    def wait_rows(step):
        up_copy(step).wait_send()
        down_copy(step).wait_recv()

        @pl.when(jnp.logical_not(bottom))
        def _():
            down_copy(step).wait_send()
            up_copy(step).wait_recv()

    def place_rows(flat, step):
        for i in range(2):
            flat[pl.ds(PADR + rows + i, planes, stride=tall), :] = get_n[
                step, pl.ds(i * planes, planes), :
            ]
        if step == 0:
            wet_flat[pl.ds(PADR + rows, levels, stride=tall), :] = get_n[
                step, pl.ds(2 * planes, levels), :
            ]

        @pl.when(bottom)
        def _():
            for i in range(2):
                flat[pl.ds(PADR - 2 + i, planes, stride=tall), :] = jnp.zeros((planes, 128), jnp.float32)
            if step == 0:
                flow_flat[pl.ds(PADR - 1, levels, stride=tall), :] = jnp.zeros((levels, 128), jnp.float32)

        @pl.when(jnp.logical_not(bottom))
        def _():
            for i in range(2):
                flat[pl.ds(PADR - 2 + i, planes, stride=tall), :] = get_s[
                    step, pl.ds(i * planes, planes), :
                ]
            if step == 0:
                flow_flat[pl.ds(PADR - 1, levels, stride=tall), :] = get_s[
                    step, pl.ds(2 * planes, levels), :
                ]

    def make_coefficients(k, g):
        at = pl.ds(PADR + 8 * g, 8)
        sub = pl.ds(8 * g, 8)
        beside = pltpu.roll(cols[tracer_count, sub, :], 126 - 4 * k, 1)
        water = wet[k, at, :]
        scale = area[sub, :] * water * (1.0 / 6.0)
        stream = east[k, sub, :] * water
        face_e = stream * pltpu.roll(jnp.where(lane == 0, beside, water), 127, 1)
        face_w = pltpu.roll(jnp.where(lane == 127, beside, stream), 1, 1) * water
        line = k * tall + PADR + 8 * g
        face_n = flow[k, at, :] * wet_flat[pl.ds(line + 1, 8), :]
        face_s = flow_flat[pl.ds(line - 1, 8), :] * water
        made = []
        centre = 1.0
        for ahead, behind in ((face_e, face_w), (face_n, face_s)):
            pos, neg = jnp.maximum(ahead, 0.0) * scale, jnp.minimum(ahead, 0.0) * scale
            pos_b, neg_b = jnp.maximum(behind, 0.0) * scale, jnp.minimum(behind, 0.0) * scale
            centre = centre - (5.0 * (pos - neg_b) + 2.0 * (neg - pos_b))
            made += [
                -pos_b,
                pos + 5.0 * pos_b + 2.0 * neg_b,
                -(2.0 * pos + 5.0 * neg + neg_b),
                neg,
            ]
        return [centre] + made

    def apply(flat, k, g, c, weights):
        centre, xm2, xm1, xp1, xp2, ym2, ym1, yp1, yp2 = weights
        base = (c * levels + k) * tall + PADR + 8 * g
        value = flat[pl.ds(pl.multiple_of(base, 8), 8), :]
        beside = pltpu.roll(cols[c, pl.ds(8 * g, 8), :], 126 - 4 * k, 1)
        total = centre * value
        total += xm2 * pltpu.roll(jnp.where(lane >= 126, beside, value), 2, 1)
        total += xm1 * pltpu.roll(jnp.where(lane == 127, beside, value), 1, 1)
        total += xp1 * pltpu.roll(jnp.where(lane == 0, beside, value), 127, 1)
        total += xp2 * pltpu.roll(jnp.where(lane <= 1, beside, value), 126, 1)
        total += ym2 * flat[pl.ds(base - 2, 8), :]
        total += ym1 * flat[pl.ds(base - 1, 8), :]
        total += yp1 * flat[pl.ds(base + 1, 8), :]
        total += yp2 * flat[pl.ds(base + 2, 8), :]
        return total

    def first_step(part):
        def level(k, acc):
            acc = list(acc)
            here = group == k
            for n, g in enumerate(parts[part]):
                weights = make_coefficients(k, g)
                for w, weight in enumerate(weights):
                    coef[k, w, pl.ds(8 * g, 8), :] = weight
                for c in range(tracer_count):
                    value = apply(first_flat, k, g, c, weights)
                    second[c * levels + k, pl.ds(PADR + 8 * g, 8), :] = value
                    i = n * tracer_count + c
                    acc[i] = jnp.where(here, pltpu.roll(value, 4 * k + 2, 1), acc[i])
            return tuple(acc)

        start = (blank,) * (tracer_count * len(parts[part]))
        return lax.fori_loop(0, levels, level, start, unroll=2)

    def second_step(part):
        def level(k, carry):
            for g in parts[part]:
                weights = [coef[k, w, pl.ds(8 * g, 8), :] for w in range(9)]
                for c in range(tracer_count):
                    final[c * levels + k, pl.ds(8 * g, 8), :] = apply(second_flat, k, g, c, weights)
            return carry

        lax.fori_loop(0, levels, level, 0, unroll=2)

    fill_rows(first_flat, 0)
    pl.semaphore_wait(barrier, n_dev - 1)
    start_rows(0)
    packed = lax.fori_loop(0, levels, gather_columns, (blank,) * ((tracer_count + 1) * groups), unroll=2)
    packed = [packed[g * (tracer_count + 1) : (g + 1) * (tracer_count + 1)] for g in range(groups)]
    for part in range(2):
        fill_columns(sum([packed[g] for g in parts[part]], ()), 0, part)
        start_columns(0, part)

    for load in loads[4:]:
        load.wait()
    cell_row, owner_row = cell[...], owner[...]
    f_row = lax.broadcasted_iota(jnp.int32, (floats, floats), 0)
    f_col = lax.broadcasted_iota(jnp.int32, (floats, floats), 1)
    diagonal = f_row == f_col
    owner_f = owner_row.astype(jnp.float32)
    owner_col = jnp.sum(jnp.where(diagonal, owner_f, 0.0), axis=1, keepdims=True)
    cell_col = jnp.sum(jnp.where(diagonal, cell_row.astype(jnp.float32), 0.0), axis=1, keepdims=True)
    rank = jnp.sum(
        jnp.where((owner_col == owner_f) & (f_col < f_row), 1.0, 0.0), axis=1, keepdims=True
    )
    slot_col = owner_col * float(BOX) + rank
    slot_lane = lax.broadcasted_iota(jnp.int32, (floats, slots), 1).astype(jnp.float32)
    wanted = jnp.sum(jnp.where(slot_col == slot_lane, cell_col + 1.0, 0.0), axis=0, keepdims=True) - 1.0
    wanted = wanted.astype(jnp.int32)
    slot_row = lax.broadcasted_iota(jnp.int32, (slots, floats), 0)
    tally = jnp.sum(
        jnp.where(owner_row * BOX + CAP == slot_row, 1.0, 0.0), axis=1, keepdims=True
    )

    def mark(r, carry):
        start = pl.multiple_of(r * 128, 128)
        place = lax.broadcasted_iota(jnp.int32, (128, slots), 0) + start
        pick[pl.ds(start, 128), :] = jnp.where(place == wanted, 1.0, 0.0).astype(jnp.bfloat16)
        return carry

    lax.fori_loop(0, rows, mark, 0)

    wait_columns(0, 0)
    place_columns(0, 0)
    packed = first_step(0)
    fill_columns(packed, 1, 0)
    start_columns(1, 0)
    wait_rows(0)
    place_rows(first_flat, 0)
    wait_columns(0, 1)
    place_columns(0, 1)
    packed = first_step(1)
    fill_rows(second_flat, 1)
    start_rows(1)
    fill_columns(packed, 1, 1)
    start_columns(1, 1)

    flat = final.reshape(planes * rows, 128)

    def take(low, high):
        for r in range(low, high):
            value = flat[pl.ds(r, planes, stride=rows), :]
            upper_half = value.astype(jnp.bfloat16)
            rest = (value - upper_half.astype(jnp.float32)).astype(jnp.bfloat16)
            halves[pl.ds(0, planes), pl.ds(r * 128, 128)] = upper_half
            halves[pl.ds(planes, planes), pl.ds(r * 128, 128)] = rest
        span = pl.ds(low * 128, (high - low) * 128)
        return jnp.dot(halves[:, span], pick[span, :], preferred_element_type=jnp.float32)

    wait_columns(1, 0)
    place_columns(1, 0)
    second_step(0)
    taken[...] = take(8, rows - 8)
    wait_rows(1)
    place_rows(second_flat, 1)
    wait_columns(1, 1)
    place_columns(1, 1)
    second_step(1)
    both = taken[...] + take(0, 8) + take(rows - 8, rows)
    outbox[...] = jnp.transpose(both[:planes] + both[planes:]) + tally

    def box_copy(j):
        other = lax.rem(me + j, n_dev)
        return pltpu.make_async_remote_copy(
            src_ref=outbox.at[pl.ds(pl.multiple_of(other * BOX, BOX), BOX)],
            dst_ref=inbox.at[pl.ds(pl.multiple_of(me * BOX, BOX), BOX)],
            send_sem=box_send.at[other],
            recv_sem=box_recv.at[me],
            device_id=(other // n_lon, lax.rem(other, n_lon)),
            device_id_type=MESH,
        )

    def box_start(j, carry):
        box_copy(j).start()
        return carry

    def box_wait(j, carry):
        other = lax.rem(me + j, n_dev)
        at = pl.ds(pl.multiple_of(other * BOX, BOX), BOX)
        copy = pltpu.make_async_remote_copy(
            src_ref=outbox.at[at],
            dst_ref=inbox.at[at],
            send_sem=box_send.at[other],
            recv_sem=box_recv.at[other],
            device_id=(other // n_lon, lax.rem(other, n_lon)),
            device_id_type=MESH,
        )
        copy.wait()
        return carry

    lax.fori_loop(1, n_dev, box_start, 0)
    own = pl.ds(pl.multiple_of(me * BOX, BOX), BOX)
    inbox[own, :] = outbox[own, :]
    lax.fori_loop(1, n_dev, box_wait, 0)
    for i in range(CAP):
        arrivals[pl.ds(i, n_dev, stride=CAP), :] = inbox[pl.ds(i, n_dev, stride=BOX), :]
    told = inbox[pl.ds(CAP, n_dev, stride=BOX), :][:, :n_dev]
    straight = lax.broadcasted_iota(jnp.int32, (n_dev, n_dev), 0) == lax.broadcasted_iota(
        jnp.int32, (n_dev, n_dev), 1
    )
    counts[...] = jnp.sum(jnp.where(straight, told, 0.0), axis=0, keepdims=True).astype(jnp.int32)


def local(tracers, vel_east, vel_north, land_mask, step_area, float_cell, float_owner):
    tracer_count, levels, rows, columns = tracers.shape
    n_lat, n_lon = lax.axis_size("lat"), lax.axis_size("lon")
    n_dev = n_lat * n_lon
    planes = tracer_count * levels
    tall = rows + 2 * PADR
    floats = float_cell.shape[0]
    row_size = 2 * planes + levels
    col_size = (tracer_count // 2 + 1) * max(rows - 16, 16)
    f32 = jnp.float32
    whole = pl.BlockSpec(memory_space=pl.ANY)
    vmem = pl.BlockSpec(memory_space=pltpu.VMEM)
    out, arrivals, counts = pl.pallas_call(
        functools.partial(kernel, (tracer_count, levels, rows, n_lat, n_lon)),
        out_shape=(
            pltpu.VMEM((planes, rows, columns), f32),
            pltpu.VMEM((n_dev * CAP, planes), f32),
            pltpu.VMEM((1, n_dev), jnp.int32),
        ),
        in_specs=[whole] * 7,
        out_specs=[vmem] * 3,
        scratch_shapes=[
            pltpu.VMEM((rows, columns), f32),
            pltpu.VMEM((1, floats), jnp.int32),
            pltpu.VMEM((1, floats), jnp.int32),
            pltpu.VMEM((levels, rows, columns), jnp.int32),
            pltpu.VMEM((levels, rows, columns), f32),
            pltpu.VMEM((levels, rows, columns), f32),
            pltpu.VMEM((planes, tall, columns), f32),
            pltpu.VMEM((planes, tall, columns), f32),
            pltpu.VMEM((levels, tall, columns), f32),
            pltpu.VMEM((levels, tall, columns), f32),
            pltpu.VMEM((levels, 9, rows, columns), f32),
            pltpu.VMEM((tracer_count + 1, rows, columns), f32),
            *[pltpu.VMEM((2, 2, col_size, columns), f32)] * 4,
            *[pltpu.VMEM((2, row_size, columns), f32)] * 4,
            pltpu.VMEM((rows * columns, n_dev * BOX), jnp.bfloat16),
            pltpu.VMEM((2 * planes, rows * columns), jnp.bfloat16),
            pltpu.VMEM((2 * planes, n_dev * BOX), f32),
            pltpu.VMEM((n_dev * BOX, planes), f32),
            pltpu.VMEM((n_dev * BOX, planes), f32),
            pltpu.SemaphoreType.DMA((7,)),
            pltpu.SemaphoreType.DMA((2, 6)),
            pltpu.SemaphoreType.DMA((2, 6)),
            pltpu.SemaphoreType.DMA((n_dev,)),
            pltpu.SemaphoreType.DMA((n_dev,)),
        ],
        compiler_params=pltpu.CompilerParams(
            collective_id=0, has_side_effects=True, vmem_limit_bytes=56 * 1024 * 1024
        ),
        cost_estimate=pl.CostEstimate(
            flops=2 * 17 * planes * rows * columns, bytes_accessed=8 * 1024 * 1024, transcendentals=0
        ),
    )(
        step_area,
        float_cell.reshape(1, floats),
        float_owner.reshape(1, floats),
        land_mask,
        vel_east,
        vel_north,
        tracers.reshape(planes, rows, columns),
    )
    return out.reshape(tracers.shape), arrivals, counts.reshape(n_dev)


def solution(mesh):
    placed = (
        P(None, None, "lat", "lon"),
        P(None, "lat", "lon"),
        P(None, "lat", "lon"),
        P(None, "lat", "lon"),
        P("lat", "lon"),
        P(("lat", "lon")),
        P(("lat", "lon"), None),
    )
    return jax.shard_map(
        local,
        mesh=mesh,
        in_specs=placed,
        out_specs=(P(None, None, "lat", "lon"), P(("lat", "lon"), None), P(("lat", "lon"))),
        check_vma=False,
    )
```

```python
import functools

import jax
import jax.numpy as jnp
from jax import lax
from jax.experimental import pallas as pl
from jax.experimental.pallas import tpu as pltpu
from jax.sharding import PartitionSpec as P

CAP = 4
BOX = 8
PADR = 8
MESH = pl.DeviceIdType.MESH


def kernel(
    dims, area_h, cell_h, owner_h, mask_h, east_h, north_h, tracers_h, final, arrivals, counts,
    area, cell, owner, mask, east, north, first, second, wet, flow, coef,
    cols, send_l, send_r, get_l, get_r, send_n, send_s, get_n, get_s,
    pick, halves, taken, outbox, inbox,
    in_sem, halo_send, halo_recv, box_send, box_recv,
):
    tracer_count, levels, rows, n_lat, n_lon = dims
    planes = tracer_count * levels
    tall = rows + 2 * PADR
    n_dev = n_lat * n_lon
    slots = n_dev * BOX
    floats = cell.shape[1]
    lat, lon = lax.axis_index("lat"), lax.axis_index("lon")
    me = lat * n_lon + lon
    top = lat == n_lat - 1
    bottom = lat == 0

    loads = [
        pltpu.make_async_copy(mask_h, mask, in_sem.at[0]),
        pltpu.make_async_copy(east_h, east, in_sem.at[1]),
        pltpu.make_async_copy(north_h, north, in_sem.at[2]),
        pltpu.make_async_copy(tracers_h, first.at[:, pl.ds(PADR, rows), :], in_sem.at[3]),
        pltpu.make_async_copy(area_h, area, in_sem.at[4]),
        pltpu.make_async_copy(cell_h, cell, in_sem.at[5]),
        pltpu.make_async_copy(owner_h, owner, in_sem.at[6]),
    ]
    for load in loads:
        load.start()

    barrier = pltpu.get_barrier_semaphore()

    def wrapped(at, step, size):
        return jnp.where(at + step >= size, at + step - size, at + step)

    lats = [wrapped(lat, i, n_lat) for i in range(n_lat)]
    lons = [wrapped(lon, i, n_lon) for i in range(n_lon)]
    others = [(a, b) for a in lats for b in lons][1:]
    for other in others:
        pl.semaphore_signal(barrier, inc=1, device_id=other, device_id_type=MESH)

    lane = lax.broadcasted_iota(jnp.int32, (8, 128), 1)
    group = lane // 4
    low_pair = lax.rem(lane, 4) < 2
    groups = rows // 8

    inner, outer = tuple(range(1, groups - 1)), (0, groups - 1)
    parts = (inner, outer)
    pairs = tracer_count // 2
    first_flat = first.reshape(planes * tall, 128)
    second_flat = second.reshape(planes * tall, 128)
    wet_flat = wet.reshape(levels * tall, 128)
    flow_flat = flow.reshape(levels * tall, 128)
    blank = jnp.zeros((8, 128), jnp.float32)

    for load in loads[:4]:
        load.wait()

    def gather_columns(k, acc):
        acc = list(acc)
        here = group == k
        for g in range(groups):
            at = pl.ds(PADR + 8 * g, 8)
            sub = pl.ds(8 * g, 8)
            water = mask[k, sub, :].astype(jnp.float32)
            wet[k, at, :] = water
            flow[k, at, :] = north[k, sub, :] * water
            edge = jnp.where(lane == 0, water, east[k, sub, :] * water)
            values = [first[c * levels + k, at, :] for c in range(tracer_count)] + [edge]
            for c, value in enumerate(values):
                i = g * (tracer_count + 1) + c
                acc[i] = jnp.where(here, pltpu.roll(value, 4 * k + 2, 1), acc[i])
        return tuple(acc)

    def fill_columns(packed, step, part):
        per = len(packed) // len(parts[part])
        for n in range(len(parts[part])):
            mine = packed[n * per : (n + 1) * per]
            for pair in range(pairs):
                a, b = mine[2 * pair], mine[2 * pair + 1]
                sub = pl.ds(pair * 8 * len(parts[part]) + 8 * n, 8)
                send_r[step, part, sub, :] = jnp.where(low_pair, a, pltpu.roll(b, 2, 1))
                send_l[step, part, sub, :] = jnp.where(low_pair, pltpu.roll(b, 126, 1), a)
            if step == 0:
                sub = pl.ds(pairs * 8 * len(parts[part]) + 8 * n, 8)
                send_r[step, part, sub, :] = mine[tracer_count]
                send_l[step, part, sub, :] = mine[tracer_count]

    def place_columns(step, part):
        for n, g in enumerate(parts[part]):
            at = pl.ds(8 * g, 8)
            for pair in range(pairs):
                sub = pl.ds(pair * 8 * len(parts[part]) + 8 * n, 8)
                from_l, from_r = get_l[step, part, sub, :], get_r[step, part, sub, :]
                cols[2 * pair, at, :] = jnp.where(low_pair, from_l, from_r)
                cols[2 * pair + 1, at, :] = jnp.where(
                    low_pair, pltpu.roll(from_l, 126, 1), pltpu.roll(from_r, 2, 1)
                )
            if step == 0:
                sub = pl.ds(pairs * 8 * len(parts[part]) + 8 * n, 8)
                cols[tracer_count, at, :] = jnp.where(
                    low_pair, get_l[step, part, sub, :], get_r[step, part, sub, :]
                )

    def fill_rows(flat, step):
        def row(r):
            return flat[pl.ds(PADR + r, planes, stride=tall), :]

        def water(r):
            line = mask.reshape(levels * rows, 128)[pl.ds(r, levels, stride=rows), :]
            return line.astype(jnp.float32)

        def stream(r):
            return north.reshape(levels * rows, 128)[pl.ds(r, levels, stride=rows), :] * water(r)

        @pl.when(jnp.logical_not(top))
        def _():
            send_n[step, pl.ds(0, planes), :] = row(rows - 2)
            send_n[step, pl.ds(planes, planes), :] = row(rows - 1)
            if step == 0:
                send_n[step, pl.ds(2 * planes, levels), :] = stream(rows - 1)

        @pl.when(top)
        def _():
            ahead = lax.broadcasted_iota(jnp.int32, (128, 128), 0)
            across = lax.broadcasted_iota(jnp.int32, (128, 128), 1)
            turn = (ahead + across == 127).astype(jnp.float32)

            def turned(value):
                return jnp.dot(
                    value, turn, precision=lax.Precision.HIGHEST, preferred_element_type=jnp.float32
                )

            send_n[step, pl.ds(0, planes), :] = turned(row(rows - 1))
            send_n[step, pl.ds(planes, planes), :] = turned(row(rows - 2))
            if step == 0:
                send_n[step, pl.ds(2 * planes, levels), :] = turned(water(rows - 1))

        send_s[step, pl.ds(0, planes), :] = row(0)
        send_s[step, pl.ds(planes, planes), :] = row(1)
        if step == 0:
            send_s[step, pl.ds(2 * planes, levels), :] = water(0)

    right, left = lax.rem(lon + 1, n_lon), lax.rem(lon + n_lon - 1, n_lon)
    upper = (jnp.where(top, lat, lat + 1), jnp.where(top, n_lon - 1 - lon, lon))
    lower = (jnp.where(bottom, 0, lat - 1), lon)

    def column_copies(step, part):
        size = (pairs + (1 if step == 0 else 0)) * 8 * len(parts[part])
        return [
            pltpu.make_async_remote_copy(
                src_ref=source.at[step, part, pl.ds(0, size)],
                dst_ref=target.at[step, part, pl.ds(0, size)],
                send_sem=halo_send.at[step, 2 * part + i],
                recv_sem=halo_recv.at[step, 2 * part + i],
                device_id=(lat, device),
                device_id_type=MESH,
            )
            for i, (source, target, device) in enumerate(
                ((send_r, get_l, right), (send_l, get_r, left))
            )
        ]

    def start_columns(step, part):
        for copy in column_copies(step, part):
            copy.start()

    def wait_columns(step, part):
        for copy in column_copies(step, part):
            copy.wait()

    def row_copy(step, source, target, out, come, device):
        size = 2 * planes + (levels if step == 0 else 0)
        return pltpu.make_async_remote_copy(
            src_ref=source.at[step, pl.ds(0, size)],
            dst_ref=target.at[step, pl.ds(0, size)],
            send_sem=halo_send.at[step, out],
            recv_sem=halo_recv.at[step, come],
            device_id=device,
            device_id_type=MESH,
        )

    def up_copy(step):
        return row_copy(step, send_n, get_s, 4, 4, upper)

    def down_copy(step):
        return row_copy(step, send_s, get_n, 5, 5, lower)

    def fold_copy(step):
        return row_copy(step, send_n, get_n, 4, 5, upper)

    def start_rows(step):
        @pl.when(top)
        def _():
            fold_copy(step).start()

        @pl.when(jnp.logical_not(top))
        def _():
            up_copy(step).start()

        @pl.when(jnp.logical_not(bottom))
        def _():
            down_copy(step).start()

    def wait_rows(step):
        up_copy(step).wait_send()
        down_copy(step).wait_recv()

        @pl.when(jnp.logical_not(bottom))
        def _():
            down_copy(step).wait_send()
            up_copy(step).wait_recv()

    def place_rows(flat, step):
        for i in range(2):
            flat[pl.ds(PADR + rows + i, planes, stride=tall), :] = get_n[
                step, pl.ds(i * planes, planes), :
            ]
        if step == 0:
            wet_flat[pl.ds(PADR + rows, levels, stride=tall), :] = get_n[
                step, pl.ds(2 * planes, levels), :
            ]

        @pl.when(bottom)
        def _():
            for i in range(2):
                flat[pl.ds(PADR - 2 + i, planes, stride=tall), :] = jnp.zeros((planes, 128), jnp.float32)
            if step == 0:
                flow_flat[pl.ds(PADR - 1, levels, stride=tall), :] = jnp.zeros((levels, 128), jnp.float32)

        @pl.when(jnp.logical_not(bottom))
        def _():
            for i in range(2):
                flat[pl.ds(PADR - 2 + i, planes, stride=tall), :] = get_s[
                    step, pl.ds(i * planes, planes), :
                ]
            if step == 0:
                flow_flat[pl.ds(PADR - 1, levels, stride=tall), :] = get_s[
                    step, pl.ds(2 * planes, levels), :
                ]

    def make_coefficients(k, g):
        at = pl.ds(PADR + 8 * g, 8)
        sub = pl.ds(8 * g, 8)
        beside = pltpu.roll(cols[tracer_count, sub, :], 126 - 4 * k, 1)
        water = wet[k, at, :]
        scale = area[sub, :] * water * (1.0 / 6.0)
        stream = east[k, sub, :] * water
        face_e = stream * pltpu.roll(jnp.where(lane == 0, beside, water), 127, 1)
        face_w = pltpu.roll(jnp.where(lane == 127, beside, stream), 1, 1) * water
        line = k * tall + PADR + 8 * g
        face_n = flow[k, at, :] * wet_flat[pl.ds(line + 1, 8), :]
        face_s = flow_flat[pl.ds(line - 1, 8), :] * water
        made = []
        centre = 1.0
        for ahead, behind in ((face_e, face_w), (face_n, face_s)):
            pos, neg = jnp.maximum(ahead, 0.0) * scale, jnp.minimum(ahead, 0.0) * scale
            pos_b, neg_b = jnp.maximum(behind, 0.0) * scale, jnp.minimum(behind, 0.0) * scale
            centre = centre - (5.0 * (pos - neg_b) + 2.0 * (neg - pos_b))
            made += [
                -pos_b,
                pos + 5.0 * pos_b + 2.0 * neg_b,
                -(2.0 * pos + 5.0 * neg + neg_b),
                neg,
            ]
        return [centre] + made

    def apply(flat, k, g, c, weights):
        centre, xm2, xm1, xp1, xp2, ym2, ym1, yp1, yp2 = weights
        base = (c * levels + k) * tall + PADR + 8 * g
        value = flat[pl.ds(pl.multiple_of(base, 8), 8), :]
        beside = pltpu.roll(cols[c, pl.ds(8 * g, 8), :], 126 - 4 * k, 1)
        total = centre * value
        total += xm2 * pltpu.roll(jnp.where(lane >= 126, beside, value), 2, 1)
        total += xm1 * pltpu.roll(jnp.where(lane == 127, beside, value), 1, 1)
        total += xp1 * pltpu.roll(jnp.where(lane == 0, beside, value), 127, 1)
        total += xp2 * pltpu.roll(jnp.where(lane <= 1, beside, value), 126, 1)
        total += ym2 * flat[pl.ds(base - 2, 8), :]
        total += ym1 * flat[pl.ds(base - 1, 8), :]
        total += yp1 * flat[pl.ds(base + 1, 8), :]
        total += yp2 * flat[pl.ds(base + 2, 8), :]
        return total

    def first_step(part):
        def level(k, acc):
            acc = list(acc)
            here = group == k
            for n, g in enumerate(parts[part]):
                weights = make_coefficients(k, g)
                for w, weight in enumerate(weights):
                    coef[k, w, pl.ds(8 * g, 8), :] = weight
                for c in range(tracer_count):
                    value = apply(first_flat, k, g, c, weights)
                    second[c * levels + k, pl.ds(PADR + 8 * g, 8), :] = value
                    i = n * tracer_count + c
                    acc[i] = jnp.where(here, pltpu.roll(value, 4 * k + 2, 1), acc[i])
            return tuple(acc)

        start = (blank,) * (tracer_count * len(parts[part]))
        return lax.fori_loop(0, levels, level, start, unroll=4)

    def second_step(part):
        def level(k, carry):
            for g in parts[part]:
                weights = [coef[k, w, pl.ds(8 * g, 8), :] for w in range(9)]
                for c in range(tracer_count):
                    final[c * levels + k, pl.ds(8 * g, 8), :] = apply(second_flat, k, g, c, weights)
            return carry

        lax.fori_loop(0, levels, level, 0, unroll=4)

    fill_rows(first_flat, 0)
    pl.semaphore_wait(barrier, n_dev - 1)
    start_rows(0)
    packed = lax.fori_loop(0, levels, gather_columns, (blank,) * ((tracer_count + 1) * groups), unroll=4)
    packed = [packed[g * (tracer_count + 1) : (g + 1) * (tracer_count + 1)] for g in range(groups)]
    for part in range(2):
        fill_columns(sum([packed[g] for g in parts[part]], ()), 0, part)
        start_columns(0, part)

    for load in loads[4:]:
        load.wait()
    cell_row, owner_row = cell[...], owner[...]
    f_row = lax.broadcasted_iota(jnp.int32, (floats, floats), 0)
    f_col = lax.broadcasted_iota(jnp.int32, (floats, floats), 1)
    diagonal = f_row == f_col
    owner_f = owner_row.astype(jnp.float32)
    owner_col = jnp.sum(jnp.where(diagonal, owner_f, 0.0), axis=1, keepdims=True)
    cell_col = jnp.sum(jnp.where(diagonal, cell_row.astype(jnp.float32), 0.0), axis=1, keepdims=True)
    rank = jnp.sum(
        jnp.where((owner_col == owner_f) & (f_col < f_row), 1.0, 0.0), axis=1, keepdims=True
    )
    slot_col = owner_col * float(BOX) + rank
    slot_lane = lax.broadcasted_iota(jnp.int32, (floats, slots), 1).astype(jnp.float32)
    wanted = jnp.sum(jnp.where(slot_col == slot_lane, cell_col + 1.0, 0.0), axis=0, keepdims=True) - 1.0
    wanted = wanted.astype(jnp.int32)
    slot_row = lax.broadcasted_iota(jnp.int32, (slots, floats), 0)
    tally = jnp.sum(
        jnp.where(owner_row * BOX + CAP == slot_row, 1.0, 0.0), axis=1, keepdims=True
    )

    def mark(r, carry):
        start = pl.multiple_of(r * 128, 128)
        place = lax.broadcasted_iota(jnp.int32, (128, slots), 0) + start
        pick[pl.ds(start, 128), :] = jnp.where(place == wanted, 1.0, 0.0).astype(jnp.bfloat16)
        return carry

    lax.fori_loop(0, rows, mark, 0, unroll=2)

    wait_columns(0, 0)
    place_columns(0, 0)
    packed = first_step(0)
    fill_columns(packed, 1, 0)
    start_columns(1, 0)
    wait_rows(0)
    place_rows(first_flat, 0)
    wait_columns(0, 1)
    place_columns(0, 1)
    packed = first_step(1)
    fill_rows(second_flat, 1)
    start_rows(1)
    fill_columns(packed, 1, 1)
    start_columns(1, 1)

    flat = final.reshape(planes * rows, 128)

    def take(low, high):
        for r in range(low, high):
            value = flat[pl.ds(r, planes, stride=rows), :]
            upper_half = value.astype(jnp.bfloat16)
            rest = (value - upper_half.astype(jnp.float32)).astype(jnp.bfloat16)
            halves[pl.ds(0, planes), pl.ds(r * 128, 128)] = upper_half
            halves[pl.ds(planes, planes), pl.ds(r * 128, 128)] = rest
        span = pl.ds(low * 128, (high - low) * 128)
        return jnp.dot(halves[:, span], pick[span, :], preferred_element_type=jnp.float32)

    wait_columns(1, 0)
    place_columns(1, 0)
    second_step(0)
    taken[...] = take(8, rows - 8)
    wait_rows(1)
    place_rows(second_flat, 1)
    wait_columns(1, 1)
    place_columns(1, 1)
    second_step(1)
    both = taken[...] + take(0, 8) + take(rows - 8, rows)
    outbox[...] = jnp.transpose(both[:planes] + both[planes:]) + tally

    own = pl.ds(pl.multiple_of(me * BOX, BOX), BOX)

    def box_copy(other, come):
        number = other[0] * n_lon + other[1]
        at = pl.ds(pl.multiple_of(number * BOX, BOX), BOX)
        return pltpu.make_async_remote_copy(
            src_ref=outbox.at[at],
            dst_ref=inbox.at[at if come else own],
            send_sem=box_send.at[number],
            recv_sem=box_recv.at[number if come else me],
            device_id=other,
            device_id_type=MESH,
        )

    for other in others:
        box_copy(other, False).start()
    inbox[own, :] = outbox[own, :]
    for other in others:
        box_copy(other, True).wait()
    for i in range(CAP):
        arrivals[pl.ds(i, n_dev, stride=CAP), :] = inbox[pl.ds(i, n_dev, stride=BOX), :]
    told = inbox[pl.ds(CAP, n_dev, stride=BOX), :][:, :n_dev]
    straight = lax.broadcasted_iota(jnp.int32, (n_dev, n_dev), 0) == lax.broadcasted_iota(
        jnp.int32, (n_dev, n_dev), 1
    )
    counts[...] = jnp.sum(jnp.where(straight, told, 0.0), axis=0, keepdims=True).astype(jnp.int32)


def local(tracers, vel_east, vel_north, land_mask, step_area, float_cell, float_owner):
    tracer_count, levels, rows, columns = tracers.shape
    n_lat, n_lon = lax.axis_size("lat"), lax.axis_size("lon")
    n_dev = n_lat * n_lon
    planes = tracer_count * levels
    tall = rows + 2 * PADR
    floats = float_cell.shape[0]
    row_size = 2 * planes + levels
    col_size = (tracer_count // 2 + 1) * max(rows - 16, 16)
    f32 = jnp.float32
    whole = pl.BlockSpec(memory_space=pl.ANY)
    vmem = pl.BlockSpec(memory_space=pltpu.VMEM)
    out, arrivals, counts = pl.pallas_call(
        functools.partial(kernel, (tracer_count, levels, rows, n_lat, n_lon)),
        out_shape=(
            pltpu.VMEM((planes, rows, columns), f32),
            pltpu.VMEM((n_dev * CAP, planes), f32),
            pltpu.VMEM((1, n_dev), jnp.int32),
        ),
        in_specs=[whole] * 7,
        out_specs=[vmem] * 3,
        scratch_shapes=[
            pltpu.VMEM((rows, columns), f32),
            pltpu.VMEM((1, floats), jnp.int32),
            pltpu.VMEM((1, floats), jnp.int32),
            pltpu.VMEM((levels, rows, columns), jnp.int32),
            pltpu.VMEM((levels, rows, columns), f32),
            pltpu.VMEM((levels, rows, columns), f32),
            pltpu.VMEM((planes, tall, columns), f32),
            pltpu.VMEM((planes, tall, columns), f32),
            pltpu.VMEM((levels, tall, columns), f32),
            pltpu.VMEM((levels, tall, columns), f32),
            pltpu.VMEM((levels, 9, rows, columns), f32),
            pltpu.VMEM((tracer_count + 1, rows, columns), f32),
            *[pltpu.VMEM((2, 2, col_size, columns), f32)] * 4,
            *[pltpu.VMEM((2, row_size, columns), f32)] * 4,
            pltpu.VMEM((rows * columns, n_dev * BOX), jnp.bfloat16),
            pltpu.VMEM((2 * planes, rows * columns), jnp.bfloat16),
            pltpu.VMEM((2 * planes, n_dev * BOX), f32),
            pltpu.VMEM((n_dev * BOX, planes), f32),
            pltpu.VMEM((n_dev * BOX, planes), f32),
            pltpu.SemaphoreType.DMA((7,)),
            pltpu.SemaphoreType.DMA((2, 6)),
            pltpu.SemaphoreType.DMA((2, 6)),
            pltpu.SemaphoreType.DMA((n_dev,)),
            pltpu.SemaphoreType.DMA((n_dev,)),
        ],
        compiler_params=pltpu.CompilerParams(
            collective_id=0, has_side_effects=True, vmem_limit_bytes=56 * 1024 * 1024
        ),
        cost_estimate=pl.CostEstimate(
            flops=2 * 17 * planes * rows * columns, bytes_accessed=8 * 1024 * 1024, transcendentals=0
        ),
    )(
        step_area,
        float_cell.reshape(1, floats),
        float_owner.reshape(1, floats),
        land_mask,
        vel_east,
        vel_north,
        tracers.reshape(planes, rows, columns),
    )
    return out.reshape(tracers.shape), arrivals, counts.reshape(n_dev)


def solution(mesh):
    placed = (
        P(None, None, "lat", "lon"),
        P(None, "lat", "lon"),
        P(None, "lat", "lon"),
        P(None, "lat", "lon"),
        P("lat", "lon"),
        P(("lat", "lon")),
        P(("lat", "lon"), None),
    )
    return jax.shard_map(
        local,
        mesh=mesh,
        in_specs=placed,
        out_specs=(P(None, None, "lat", "lon"), P(("lat", "lon"), None), P(("lat", "lon"))),
        check_vma=False,
    )
```

```python
import functools

import jax
import jax.numpy as jnp
from jax import lax
from jax.experimental import pallas as pl
from jax.experimental.pallas import tpu as pltpu
from jax.sharding import PartitionSpec as P

CAP = 4
BOX = 8
PADR = 8
MESH = pl.DeviceIdType.MESH


def kernel(
    dims, area_h, cell_h, owner_h, mask_h, east_h, north_h, tracers_h, final, arrivals, counts,
    area, cell, owner, mask, east, north, field, wet, flow, coef,
    pack, cols, send_l, send_r, get_l, get_r, send_n, send_s, get_n, get_s,
    pick, taken, outbox, inbox,
    in_sem, out_sem, halo_send, halo_recv, box_send, box_recv,
):
    tracer_count, levels, rows, n_lat, n_lon = dims
    planes = tracer_count * levels
    tall = rows + 2 * PADR
    n_dev = n_lat * n_lon
    slots = n_dev * BOX
    floats = cell.shape[1]
    groups = rows // 8
    wide = groups // 2
    pairs = tracer_count // 2
    lat, lon = lax.axis_index("lat"), lax.axis_index("lon")
    me = lat * n_lon + lon
    top = lat == n_lat - 1
    bottom = lat == 0

    loads = [
        pltpu.make_async_copy(mask_h, mask, in_sem.at[0]),
        pltpu.make_async_copy(east_h, east, in_sem.at[1]),
        pltpu.make_async_copy(north_h, north, in_sem.at[2]),
        pltpu.make_async_copy(tracers_h, field.at[0, :, pl.ds(PADR, rows), :], in_sem.at[3]),
        pltpu.make_async_copy(area_h, area, in_sem.at[4]),
        pltpu.make_async_copy(cell_h, cell, in_sem.at[5]),
        pltpu.make_async_copy(owner_h, owner, in_sem.at[6]),
    ]
    for load in loads:
        load.start()

    barrier = pltpu.get_barrier_semaphore()

    def device(number):
        return (lax.div(number, n_lon), lax.rem(number, n_lon))

    def after_me(j):
        return jnp.where(me + j >= n_dev, me + j - n_dev, me + j)

    def greet(j, carry):
        pl.semaphore_signal(barrier, inc=1, device_id=device(after_me(j)), device_id_type=MESH)
        return carry

    lax.fori_loop(1, n_dev, greet, 0)

    lane = lax.broadcasted_iota(jnp.int32, (8, 128), 1)
    group = lane // 4
    low_pair = lax.rem(lane, 4) < 2
    flat = field.reshape(3 * planes * tall, 128)
    wet_flat = wet.reshape(levels * tall, 128)
    flow_flat = flow.reshape(levels * tall, 128)
    mask_flat = mask.reshape(levels * rows, 128)
    north_flat = north.reshape(levels * rows, 128)

    def group_of(part, n):
        if n < wide // 2:
            return n + jnp.where(part == 0, wide // 2, 0)
        return n + jnp.where(part == 0, wide // 2, wide)

    def eight(start):
        return pl.ds(pl.multiple_of(start, 8), 8)

    for load in loads:
        load.wait()

    def gather_columns(k, acc):
        acc = list(acc)
        here = group == k
        for g in range(groups):
            at = pl.ds(PADR + 8 * g, 8)
            sub = pl.ds(8 * g, 8)
            water = mask[k, sub, :].astype(jnp.float32)
            wet[k, at, :] = water
            flow[k, at, :] = north[k, sub, :] * water
            edge = jnp.where(lane == 0, water, east[k, sub, :] * water)
            values = [field[0, c * levels + k, at, :] for c in range(tracer_count)] + [edge]
            for c, value in enumerate(values):
                i = c * groups + g
                acc[i] = jnp.where(here, pltpu.roll(value, 4 * k + 2, 1), acc[i])
        return tuple(acc)

    right, left = lax.rem(lon + 1, n_lon), lax.rem(lon + n_lon - 1, n_lon)
    upper = (jnp.where(top, lat, lat + 1), jnp.where(top, n_lon - 1 - lon, lon))
    lower = (jnp.where(bottom, 0, lat - 1), lon)

    def column_copy(step, part, i):
        source, target, to = ((send_r, get_l, right), (send_l, get_r, left))[i]
        return pltpu.make_async_remote_copy(
            src_ref=source.at[step, part],
            dst_ref=target.at[step, part],
            send_sem=halo_send.at[step, 2 * part + i],
            recv_sem=halo_recv.at[step, 2 * part + i],
            device_id=(lat, to),
            device_id_type=MESH,
        )

    def send_columns(step, part):
        for n in range(wide):
            at = eight(8 * group_of(part, n))
            for pair in range(pairs):
                a, b = pack[2 * pair, at, :], pack[2 * pair + 1, at, :]
                sub = pl.ds((pair * wide + n) * 8, 8)
                send_r[step, part, sub, :] = jnp.where(low_pair, a, pltpu.roll(b, 2, 1))
                send_l[step, part, sub, :] = jnp.where(low_pair, pltpu.roll(b, 126, 1), a)
            sub = pl.ds((pairs * wide + n) * 8, 8)
            send_r[step, part, sub, :] = pack[tracer_count, at, :]
            send_l[step, part, sub, :] = pack[tracer_count, at, :]
        column_copy(step, part, 0).start()
        column_copy(step, part, 1).start()

    def take_columns(step, part):
        column_copy(step, part, 0).wait()
        column_copy(step, part, 1).wait()
        for n in range(wide):
            at = eight(8 * group_of(part, n))
            for pair in range(pairs):
                sub = pl.ds((pair * wide + n) * 8, 8)
                from_l, from_r = get_l[step, part, sub, :], get_r[step, part, sub, :]
                cols[2 * pair, at, :] = jnp.where(low_pair, from_l, from_r)
                cols[2 * pair + 1, at, :] = jnp.where(
                    low_pair, pltpu.roll(from_l, 126, 1), pltpu.roll(from_r, 2, 1)
                )
            sub = pl.ds((pairs * wide + n) * 8, 8)
            cols[tracer_count, at, :] = jnp.where(
                low_pair, get_l[step, part, sub, :], get_r[step, part, sub, :]
            )

    def row_copy(step, source, target, out, come, to):
        return pltpu.make_async_remote_copy(
            src_ref=source.at[step],
            dst_ref=target.at[step],
            send_sem=halo_send.at[step, out],
            recv_sem=halo_recv.at[step, come],
            device_id=to,
            device_id_type=MESH,
        )

    def up_copy(step):
        return row_copy(step, send_n, get_s, 4, 4, upper)

    def down_copy(step):
        return row_copy(step, send_s, get_n, 5, 5, lower)

    def fold_copy(step):
        return row_copy(step, send_n, get_n, 4, 5, upper)

    def send_rows(step):
        start = step * (planes * tall) + PADR

        def row(r):
            return flat[pl.ds(start + r, planes, stride=tall), :]

        send_s[step, pl.ds(0, planes), :] = row(0)
        send_s[step, pl.ds(planes, planes), :] = row(1)
        send_s[step, pl.ds(2 * planes, levels), :] = mask_flat[
            pl.ds(0, levels, stride=rows), :
        ].astype(jnp.float32)

        @pl.when(jnp.logical_not(bottom))
        def _():
            down_copy(step).start()

        last, before = row(rows - 1), row(rows - 2)
        edge = pl.ds(rows - 1, levels, stride=rows)
        water = mask_flat[edge, :].astype(jnp.float32)
        send_n[step, pl.ds(0, planes), :] = jnp.where(top, last, before)
        send_n[step, pl.ds(planes, planes), :] = jnp.where(top, before, last)
        send_n[step, pl.ds(2 * planes, levels), :] = water * jnp.where(top, 1.0, north_flat[edge, :])

        @pl.when(top)
        def _():
            ahead = lax.broadcasted_iota(jnp.int32, (128, 128), 0)
            across = lax.broadcasted_iota(jnp.int32, (128, 128), 1)
            turn = (ahead + across == 127).astype(jnp.float32)

            def reverse(i, carry):
                at = pl.ds(pl.multiple_of(i * levels, levels), levels)
                send_n[step, at, :] = jnp.dot(
                    send_n[step, at, :],
                    turn,
                    precision=lax.Precision.HIGHEST,
                    preferred_element_type=jnp.float32,
                )
                return carry

            lax.fori_loop(0, 2 * tracer_count + 1, reverse, 0)
            fold_copy(step).start()

        @pl.when(jnp.logical_not(top))
        def _():
            up_copy(step).start()

    def take_rows(step):
        up_copy(step).wait_send()
        down_copy(step).wait_recv()
        start = step * (planes * tall) + PADR
        for i in range(2):
            flat[pl.ds(start + rows + i, planes, stride=tall), :] = get_n[
                step, pl.ds(i * planes, planes), :
            ]
        wet_flat[pl.ds(PADR + rows, levels, stride=tall), :] = get_n[
            step, pl.ds(2 * planes, levels), :
        ]

        @pl.when(bottom)
        def _():
            get_s[step] = jnp.zeros((2 * planes + levels, 128), jnp.float32)

        @pl.when(jnp.logical_not(bottom))
        def _():
            down_copy(step).wait_send()
            up_copy(step).wait_recv()

        for i in range(2):
            flat[pl.ds(start - 2 + i, planes, stride=tall), :] = get_s[
                step, pl.ds(i * planes, planes), :
            ]
        flow_flat[pl.ds(PADR - 1, levels, stride=tall), :] = get_s[step, pl.ds(2 * planes, levels), :]

    def make_coefficients(k, g):
        at = eight(PADR + 8 * g)
        sub = eight(8 * g)
        line = k * tall + PADR + 8 * g
        beside = pltpu.roll(cols[tracer_count, sub, :], 126 - 4 * k, 1)
        water = wet[k, at, :]
        scale = area[sub, :] * water * (1.0 / 6.0)
        stream = east[k, sub, :] * water
        face_e = stream * pltpu.roll(jnp.where(lane == 0, beside, water), 127, 1)
        face_w = pltpu.roll(jnp.where(lane == 127, beside, stream), 1, 1) * water
        face_n = flow[k, at, :] * wet_flat[pl.ds(line + 1, 8), :]
        face_s = flow_flat[pl.ds(line - 1, 8), :] * water
        made = []
        centre = 1.0
        for ahead, behind in ((face_e, face_w), (face_n, face_s)):
            pos, neg = jnp.maximum(ahead, 0.0) * scale, jnp.minimum(ahead, 0.0) * scale
            pos_b, neg_b = jnp.maximum(behind, 0.0) * scale, jnp.minimum(behind, 0.0) * scale
            centre = centre - (5.0 * (pos - neg_b) + 2.0 * (neg - pos_b))
            made += [
                -pos_b,
                pos + 5.0 * pos_b + 2.0 * neg_b,
                -(2.0 * pos + 5.0 * neg + neg_b),
                neg,
            ]
        for w, weight in enumerate([centre] + made):
            coef[k, w, sub, :] = weight

    def apply(base, beside, weights):
        centre, xm2, xm1, xp1, xp2, ym2, ym1, yp1, yp2 = weights
        value = flat[eight(base), :]
        total = centre * value
        total += xm2 * pltpu.roll(jnp.where(lane >= 126, beside, value), 2, 1)
        total += xm1 * pltpu.roll(jnp.where(lane == 127, beside, value), 1, 1)
        total += xp1 * pltpu.roll(jnp.where(lane == 0, beside, value), 127, 1)
        total += xp2 * pltpu.roll(jnp.where(lane <= 1, beside, value), 126, 1)
        total += ym2 * flat[pl.ds(base - 2, 8), :]
        total += ym1 * flat[pl.ds(base - 1, 8), :]
        total += yp1 * flat[pl.ds(base + 1, 8), :]
        total += yp2 * flat[pl.ds(base + 2, 8), :]
        return total

    def run_part(step, part):
        @pl.when(step == 0)
        def _():
            def level(k, carry):
                for n in range(wide):
                    make_coefficients(k, group_of(part, n))
                return carry

            lax.fori_loop(0, levels, level, 0)

        def level(k, acc):
            acc = list(acc)
            here = group == k
            for n in range(wide):
                g = group_of(part, n)
                sub = eight(8 * g)
                weights = [coef[k, w, sub, :] for w in range(9)]
                for c in range(tracer_count):
                    base = (step * planes + c * levels + k) * tall + PADR + 8 * g
                    beside = pltpu.roll(cols[c, sub, :], 126 - 4 * k, 1)
                    value = apply(base, beside, weights)
                    flat[eight(base + planes * tall), :] = value
                    i = n * tracer_count + c
                    acc[i] = jnp.where(here, pltpu.roll(value, 4 * k + 2, 1), acc[i])
            return tuple(acc)

        packed = lax.fori_loop(0, levels, level, (blank,) * (tracer_count * wide))
        for n in range(wide):
            for c in range(tracer_count):
                pack[c, eight(8 * group_of(part, n)), :] = packed[n * tracer_count + c]

    def take_cells(part):
        def two_rows(i, carry):
            r = 2 * jnp.where(part == 0, rows // 8 + i, jnp.where(i < rows // 8, i, i + rows // 4))
            start = 2 * planes * tall + PADR + r
            value = jnp.concatenate(
                [flat[pl.ds(start + h, planes, stride=tall), :] for h in range(2)], axis=1
            )
            high = value.astype(jnp.bfloat16)
            rest = (value - high.astype(jnp.float32)).astype(jnp.bfloat16)
            chosen = pick[pl.ds(pl.multiple_of(r * 128, 256), 256), :]
            taken[...] += jnp.dot(
                jnp.concatenate([high, rest], axis=0), chosen, preferred_element_type=jnp.float32
            )
            return carry

        lax.fori_loop(0, rows // 4, two_rows, 0)

    blank = jnp.zeros((8, 128), jnp.float32)
    packed = lax.fori_loop(0, levels, gather_columns, (blank,) * ((tracer_count + 1) * groups))
    for i, value in enumerate(packed):
        pack[i // groups, pl.ds(8 * (i % groups), 8), :] = value
    pl.semaphore_wait(barrier, n_dev - 1)

    def first_columns(part, carry):
        send_columns(0, part)
        return carry

    lax.fori_loop(0, 2, first_columns, 0)

    def one_step(step, carry):
        send_rows(step)

        @pl.when(step == 0)
        def _():
            prepare()

        def one_part(part, carry):
            take_columns(step, part)

            @pl.when(part == 1)
            def _():
                take_rows(step)

            run_part(step, part)

            @pl.when(step == 0)
            def _():
                send_columns(1, part)

            @pl.when(step == 1)
            def _():
                take_cells(part)

            return carry

        lax.fori_loop(0, 2, one_part, 0)
        return carry

    f_row = lax.broadcasted_iota(jnp.int32, (floats, floats), 0)
    f_col = lax.broadcasted_iota(jnp.int32, (floats, floats), 1)
    owner_row = owner[...]

    def prepare():
        diagonal = f_row == f_col
        cell_f, owner_f = cell[...].astype(jnp.float32), owner_row.astype(jnp.float32)
        owner_col = jnp.sum(jnp.where(diagonal, owner_f, 0.0), axis=1, keepdims=True)
        cell_col = jnp.sum(jnp.where(diagonal, cell_f, 0.0), axis=1, keepdims=True)
        rank = jnp.sum(
            jnp.where((owner_col == owner_f) & (f_col < f_row), 1.0, 0.0), axis=1, keepdims=True
        )
        slot_col = owner_col * float(BOX) + rank
        slot_lane = lax.broadcasted_iota(jnp.int32, (floats, slots), 1).astype(jnp.float32)
        wanted = jnp.sum(jnp.where(slot_col == slot_lane, cell_col + 1.0, 0.0), axis=0, keepdims=True)
        wanted = wanted.astype(jnp.int32) - 1
        taken[...] = jnp.zeros_like(taken)

        def mark(r, carry):
            start = pl.multiple_of(r * 32, 32)
            place = lax.broadcasted_iota(jnp.int32, (32, slots), 0) + start
            pick[pl.ds(start, 32), :] = jnp.where(place == wanted, 1.0, 0.0).astype(jnp.bfloat16)
            return carry

        lax.fori_loop(0, rows * 4, mark, 0)

    lax.fori_loop(0, 2, one_step, 0)
    store = pltpu.make_async_copy(field.at[2, :, pl.ds(PADR, rows), :], final, out_sem.at[0])
    store.start()

    slot_row = lax.broadcasted_iota(jnp.int32, (slots, floats), 0)
    tally = jnp.sum(jnp.where(owner_row * BOX + CAP == slot_row, 1.0, 0.0), axis=1, keepdims=True)
    outbox[...] = jnp.transpose(taken[pl.ds(0, planes), :] + taken[pl.ds(planes, planes), :]) + tally
    own = pl.ds(pl.multiple_of(me * BOX, BOX), BOX)

    def box_copy(j, come):
        other = after_me(j)
        at = pl.ds(pl.multiple_of(other * BOX, BOX), BOX)
        return pltpu.make_async_remote_copy(
            src_ref=outbox.at[at],
            dst_ref=inbox.at[at if come else own],
            send_sem=box_send.at[other],
            recv_sem=box_recv.at[other if come else me],
            device_id=device(other),
            device_id_type=MESH,
        )

    def box_start(j, carry):
        box_copy(j, False).start()
        return carry

    def box_wait(j, carry):
        box_copy(j, True).wait()
        return carry

    lax.fori_loop(1, n_dev, box_start, 0)
    inbox[own, :] = outbox[own, :]
    lax.fori_loop(1, n_dev, box_wait, 0)
    for i in range(CAP):
        arrivals[pl.ds(i, n_dev, stride=CAP), :] = inbox[pl.ds(i, n_dev, stride=BOX), :]
    told = inbox[pl.ds(CAP, n_dev, stride=BOX), :][:, :n_dev]
    straight = lax.broadcasted_iota(jnp.int32, (n_dev, n_dev), 0) == lax.broadcasted_iota(
        jnp.int32, (n_dev, n_dev), 1
    )
    counts[...] = jnp.sum(jnp.where(straight, told, 0.0), axis=0, keepdims=True).astype(jnp.int32)
    store.wait()


def local(tracers, vel_east, vel_north, land_mask, step_area, float_cell, float_owner):
    tracer_count, levels, rows, columns = tracers.shape
    n_lat, n_lon = lax.axis_size("lat"), lax.axis_size("lon")
    n_dev = n_lat * n_lon
    planes = tracer_count * levels
    tall = rows + 2 * PADR
    floats = float_cell.shape[0]
    row_size = 2 * planes + levels
    col_size = (tracer_count // 2 + 1) * rows // 2
    f32 = jnp.float32
    whole = pl.BlockSpec(memory_space=pl.ANY)
    vmem = pl.BlockSpec(memory_space=pltpu.VMEM)
    out, arrivals, counts = pl.pallas_call(
        functools.partial(kernel, (tracer_count, levels, rows, n_lat, n_lon)),
        out_shape=(
            pltpu.VMEM((planes, rows, columns), f32),
            pltpu.VMEM((n_dev * CAP, planes), f32),
            pltpu.VMEM((1, n_dev), jnp.int32),
        ),
        in_specs=[whole] * 7,
        out_specs=[vmem] * 3,
        scratch_shapes=[
            pltpu.VMEM((rows, columns), f32),
            pltpu.VMEM((1, floats), jnp.int32),
            pltpu.VMEM((1, floats), jnp.int32),
            pltpu.VMEM((levels, rows, columns), jnp.int32),
            pltpu.VMEM((levels, rows, columns), f32),
            pltpu.VMEM((levels, rows, columns), f32),
            pltpu.VMEM((3, planes, tall, columns), f32),
            pltpu.VMEM((levels, tall, columns), f32),
            pltpu.VMEM((levels, tall, columns), f32),
            pltpu.VMEM((levels, 9, rows, columns), f32),
            *[pltpu.VMEM((tracer_count + 1, rows, columns), f32)] * 2,
            *[pltpu.VMEM((2, 2, col_size, columns), f32)] * 4,
            *[pltpu.VMEM((2, row_size, columns), f32)] * 4,
            pltpu.VMEM((rows * columns, n_dev * BOX), jnp.bfloat16),
            pltpu.VMEM((2 * planes, n_dev * BOX), f32),
            pltpu.VMEM((n_dev * BOX, planes), f32),
            pltpu.VMEM((n_dev * BOX, planes), f32),
            pltpu.SemaphoreType.DMA((7,)),
            pltpu.SemaphoreType.DMA((1,)),
            pltpu.SemaphoreType.DMA((2, 6)),
            pltpu.SemaphoreType.DMA((2, 6)),
            pltpu.SemaphoreType.DMA((n_dev,)),
            pltpu.SemaphoreType.DMA((n_dev,)),
        ],
        compiler_params=pltpu.CompilerParams(
            collective_id=0, has_side_effects=True, vmem_limit_bytes=56 * 1024 * 1024
        ),
        cost_estimate=pl.CostEstimate(
            flops=2 * 17 * planes * rows * columns, bytes_accessed=8 * 1024 * 1024, transcendentals=0
        ),
    )(
        step_area,
        float_cell.reshape(1, floats),
        float_owner.reshape(1, floats),
        land_mask,
        vel_east,
        vel_north,
        tracers.reshape(planes, rows, columns),
    )
    return out.reshape(tracers.shape), arrivals, counts.reshape(n_dev)


def solution(mesh):
    placed = (
        P(None, None, "lat", "lon"),
        P(None, "lat", "lon"),
        P(None, "lat", "lon"),
        P(None, "lat", "lon"),
        P("lat", "lon"),
        P(("lat", "lon")),
        P(("lat", "lon"), None),
    )
    return jax.shard_map(
        local,
        mesh=mesh,
        in_specs=placed,
        out_specs=(P(None, None, "lat", "lon"), P(("lat", "lon"), None), P(("lat", "lon"))),
        check_vma=False,
    )
```

```python
import functools

import jax
import jax.numpy as jnp
from jax import lax
from jax.experimental import pallas as pl
from jax.experimental.pallas import tpu as pltpu
from jax.sharding import PartitionSpec as P

CAP = 4
BOX = 8
PADR = 8
MESH = pl.DeviceIdType.MESH


def kernel(
    dims, area_h, cell_h, owner_h, mask_h, east_h, north_h, tracers_h, final, arrivals, counts,
    area, cell, owner, mask, east, north, first, second, wet, flow, coef,
    cols, send_l, send_r, get_l, get_r, send_n, send_s, get_n, get_s,
    pick, halves, taken, outbox, inbox,
    in_sem, halo_send, halo_recv, box_send, box_recv,
):
    tracer_count, levels, rows, n_lat, n_lon = dims
    planes = tracer_count * levels
    tall = rows + 2 * PADR
    n_dev = n_lat * n_lon
    slots = n_dev * BOX
    floats = cell.shape[1]
    lat, lon = lax.axis_index("lat"), lax.axis_index("lon")
    me = lat * n_lon + lon
    top = lat == n_lat - 1
    bottom = lat == 0

    loads = [
        pltpu.make_async_copy(mask_h, mask, in_sem.at[0]),
        pltpu.make_async_copy(east_h, east, in_sem.at[1]),
        pltpu.make_async_copy(north_h, north, in_sem.at[2]),
        pltpu.make_async_copy(tracers_h, first.at[:, pl.ds(PADR, rows), :], in_sem.at[3]),
        pltpu.make_async_copy(area_h, area, in_sem.at[4]),
        pltpu.make_async_copy(cell_h, cell, in_sem.at[5]),
        pltpu.make_async_copy(owner_h, owner, in_sem.at[6]),
    ]
    for load in loads:
        load.start()

    barrier = pltpu.get_barrier_semaphore()

    def greet(j, carry):
        other = lax.rem(me + j, n_dev)
        pl.semaphore_signal(
            barrier, inc=1, device_id=(other // n_lon, lax.rem(other, n_lon)), device_id_type=MESH
        )
        return carry

    lax.fori_loop(1, n_dev, greet, 0)

    lane = lax.broadcasted_iota(jnp.int32, (8, 128), 1)
    group = lane // 4
    low_pair = lax.rem(lane, 4) < 2
    groups = rows // 8

    inner, outer = tuple(range(1, groups - 1)), (0, groups - 1)
    parts = (inner, outer)
    pairs = tracer_count // 2
    first_flat = first.reshape(planes * tall, 128)
    second_flat = second.reshape(planes * tall, 128)
    wet_flat = wet.reshape(levels * tall, 128)
    flow_flat = flow.reshape(levels * tall, 128)
    blank = jnp.zeros((8, 128), jnp.float32)

    for load in loads[:4]:
        load.wait()

    def gather_columns(k, acc):
        acc = list(acc)
        here = group == k
        for g in range(groups):
            at = pl.ds(PADR + 8 * g, 8)
            sub = pl.ds(8 * g, 8)
            water = mask[k, sub, :].astype(jnp.float32)
            wet[k, at, :] = water
            flow[k, at, :] = north[k, sub, :] * water
            edge = jnp.where(lane == 0, water, east[k, sub, :] * water)
            values = [first[c * levels + k, at, :] for c in range(tracer_count)] + [edge]
            for c, value in enumerate(values):
                i = g * (tracer_count + 1) + c
                acc[i] = jnp.where(here, pltpu.roll(value, 4 * k + 2, 1), acc[i])
        return tuple(acc)

    def fill_columns(packed, step, part):
        per = len(packed) // len(parts[part])
        for n in range(len(parts[part])):
            mine = packed[n * per : (n + 1) * per]
            for pair in range(pairs):
                a, b = mine[2 * pair], mine[2 * pair + 1]
                sub = pl.ds(pair * 8 * len(parts[part]) + 8 * n, 8)
                send_r[step, part, sub, :] = jnp.where(low_pair, a, pltpu.roll(b, 2, 1))
                send_l[step, part, sub, :] = jnp.where(low_pair, pltpu.roll(b, 126, 1), a)
            if step == 0:
                sub = pl.ds(pairs * 8 * len(parts[part]) + 8 * n, 8)
                send_r[step, part, sub, :] = mine[tracer_count]
                send_l[step, part, sub, :] = mine[tracer_count]

    def place_columns(step, part):
        for n, g in enumerate(parts[part]):
            at = pl.ds(8 * g, 8)
            for pair in range(pairs):
                sub = pl.ds(pair * 8 * len(parts[part]) + 8 * n, 8)
                from_l, from_r = get_l[step, part, sub, :], get_r[step, part, sub, :]
                cols[2 * pair, at, :] = jnp.where(low_pair, from_l, from_r)
                cols[2 * pair + 1, at, :] = jnp.where(
                    low_pair, pltpu.roll(from_l, 126, 1), pltpu.roll(from_r, 2, 1)
                )
            if step == 0:
                sub = pl.ds(pairs * 8 * len(parts[part]) + 8 * n, 8)
                cols[tracer_count, at, :] = jnp.where(
                    low_pair, get_l[step, part, sub, :], get_r[step, part, sub, :]
                )

    def fill_rows(flat, step):
        def row(r):
            return flat[pl.ds(PADR + r, planes, stride=tall), :]

        def water(r):
            line = mask.reshape(levels * rows, 128)[pl.ds(r, levels, stride=rows), :]
            return line.astype(jnp.float32)

        def stream(r):
            return north.reshape(levels * rows, 128)[pl.ds(r, levels, stride=rows), :] * water(r)

        last, before = row(rows - 1), row(rows - 2)
        send_n[step, pl.ds(0, planes), :] = jnp.where(top, last, before)
        send_n[step, pl.ds(planes, planes), :] = jnp.where(top, before, last)
        if step == 0:
            send_n[step, pl.ds(2 * planes, levels), :] = jnp.where(
                top, water(rows - 1), stream(rows - 1)
            )

        @pl.when(top)
        def _():
            ahead = lax.broadcasted_iota(jnp.int32, (128, 128), 0)
            across = lax.broadcasted_iota(jnp.int32, (128, 128), 1)
            turn = (ahead + across == 127).astype(jnp.float32)

            def reverse(i, carry):
                at = pl.ds(pl.multiple_of(i * levels, levels), levels)
                send_n[step, at, :] = jnp.dot(
                    send_n[step, at, :],
                    turn,
                    precision=lax.Precision.HIGHEST,
                    preferred_element_type=jnp.float32,
                )
                return carry

            lax.fori_loop(0, 2 * tracer_count + (1 if step == 0 else 0), reverse, 0)

        send_s[step, pl.ds(0, planes), :] = row(0)
        send_s[step, pl.ds(planes, planes), :] = row(1)
        if step == 0:
            send_s[step, pl.ds(2 * planes, levels), :] = water(0)

    right, left = lax.rem(lon + 1, n_lon), lax.rem(lon + n_lon - 1, n_lon)
    upper = (jnp.where(top, lat, lat + 1), jnp.where(top, n_lon - 1 - lon, lon))
    lower = (jnp.where(bottom, 0, lat - 1), lon)

    def column_copies(step, part):
        size = (pairs + (1 if step == 0 else 0)) * 8 * len(parts[part])
        return [
            pltpu.make_async_remote_copy(
                src_ref=source.at[step, part, pl.ds(0, size)],
                dst_ref=target.at[step, part, pl.ds(0, size)],
                send_sem=halo_send.at[step, 2 * part + i],
                recv_sem=halo_recv.at[step, 2 * part + i],
                device_id=(lat, device),
                device_id_type=MESH,
            )
            for i, (source, target, device) in enumerate(
                ((send_r, get_l, right), (send_l, get_r, left))
            )
        ]

    def start_columns(step, part):
        for copy in column_copies(step, part):
            copy.start()

    def wait_columns(step, part):
        for copy in column_copies(step, part):
            copy.wait()

    def row_copy(step, source, target, out, come, device):
        size = 2 * planes + (levels if step == 0 else 0)
        return pltpu.make_async_remote_copy(
            src_ref=source.at[step, pl.ds(0, size)],
            dst_ref=target.at[step, pl.ds(0, size)],
            send_sem=halo_send.at[step, out],
            recv_sem=halo_recv.at[step, come],
            device_id=device,
            device_id_type=MESH,
        )

    def up_copy(step):
        return row_copy(step, send_n, get_s, 4, 4, upper)

    def down_copy(step):
        return row_copy(step, send_s, get_n, 5, 5, lower)

    def fold_copy(step):
        return row_copy(step, send_n, get_n, 4, 5, upper)

    def start_rows(step):
        @pl.when(top)
        def _():
            fold_copy(step).start()

        @pl.when(jnp.logical_not(top))
        def _():
            up_copy(step).start()

        @pl.when(jnp.logical_not(bottom))
        def _():
            down_copy(step).start()

    def wait_rows(step):
        up_copy(step).wait_send()
        down_copy(step).wait_recv()

        @pl.when(jnp.logical_not(bottom))
        def _():
            down_copy(step).wait_send()
            up_copy(step).wait_recv()

    def place_rows(flat, step):
        for i in range(2):
            flat[pl.ds(PADR + rows + i, planes, stride=tall), :] = get_n[
                step, pl.ds(i * planes, planes), :
            ]
        if step == 0:
            wet_flat[pl.ds(PADR + rows, levels, stride=tall), :] = get_n[
                step, pl.ds(2 * planes, levels), :
            ]

        @pl.when(bottom)
        def _():
            for i in range(2):
                flat[pl.ds(PADR - 2 + i, planes, stride=tall), :] = jnp.zeros((planes, 128), jnp.float32)
            if step == 0:
                flow_flat[pl.ds(PADR - 1, levels, stride=tall), :] = jnp.zeros((levels, 128), jnp.float32)

        @pl.when(jnp.logical_not(bottom))
        def _():
            for i in range(2):
                flat[pl.ds(PADR - 2 + i, planes, stride=tall), :] = get_s[
                    step, pl.ds(i * planes, planes), :
                ]
            if step == 0:
                flow_flat[pl.ds(PADR - 1, levels, stride=tall), :] = get_s[
                    step, pl.ds(2 * planes, levels), :
                ]

    def make_coefficients(k, g, beside):
        at = pl.ds(PADR + 8 * g, 8)
        sub = pl.ds(8 * g, 8)
        water = wet[k, at, :]
        scale = area[sub, :] * water * (1.0 / 6.0)
        stream = east[k, sub, :] * water
        face_e = stream * pltpu.roll(jnp.where(lane == 0, beside, water), 127, 1)
        face_w = pltpu.roll(jnp.where(lane == 127, beside, stream), 1, 1) * water
        line = k * tall + PADR + 8 * g
        face_n = flow[k, at, :] * wet_flat[pl.ds(line + 1, 8), :]
        face_s = flow_flat[pl.ds(line - 1, 8), :] * water
        made = []
        centre = 1.0
        for ahead, behind in ((face_e, face_w), (face_n, face_s)):
            pos, neg = jnp.maximum(ahead, 0.0) * scale, jnp.minimum(ahead, 0.0) * scale
            pos_b, neg_b = jnp.maximum(behind, 0.0) * scale, jnp.minimum(behind, 0.0) * scale
            centre = centre - (5.0 * (pos - neg_b) + 2.0 * (neg - pos_b))
            made += [
                -pos_b,
                pos + 5.0 * pos_b + 2.0 * neg_b,
                -(2.0 * pos + 5.0 * neg + neg_b),
                neg,
            ]
        return [centre] + made

    def sides_of(part, k, count):
        shift = (126 - 4 * k) & 127
        return tuple(
            pltpu.roll(cols[c, pl.ds(8 * g, 8), :], shift, 1) for g in parts[part] for c in range(count)
        )

    def apply(flat, k, g, c, weights, beside):
        centre, xm2, xm1, xp1, xp2, ym2, ym1, yp1, yp2 = weights
        base = (c * levels + k) * tall + PADR + 8 * g
        value = flat[pl.ds(pl.multiple_of(base, 8), 8), :]
        total = centre * value
        total += ym2 * flat[pl.ds(base - 2, 8), :]
        total += ym1 * flat[pl.ds(base - 1, 8), :]
        total += yp1 * flat[pl.ds(base + 1, 8), :]
        total += yp2 * flat[pl.ds(base + 2, 8), :]
        total += xm2 * pltpu.roll(jnp.where(lane >= 126, beside, value), 2, 1)
        total += xm1 * pltpu.roll(jnp.where(lane == 127, beside, value), 1, 1)
        total += xp1 * pltpu.roll(jnp.where(lane == 0, beside, value), 127, 1)
        total += xp2 * pltpu.roll(jnp.where(lane <= 1, beside, value), 126, 1)
        return total

    def first_step(part):
        count = tracer_count + 1

        def pack(acc, done, k):
            here = group == k
            shift = (4 * k + 2) & 127
            return tuple(jnp.where(here, pltpu.roll(v, shift, 1), a) for a, v in zip(acc, done))

        def level(k, carry):
            acc, done, sides = carry
            acc = pack(acc, done, k - 1)
            ahead = sides_of(part, k + 1, count)
            done = []
            for n, g in enumerate(parts[part]):
                weights = make_coefficients(k, g, sides[n * count + tracer_count])
                for w, weight in enumerate(weights):
                    coef[k, w, pl.ds(8 * g, 8), :] = weight
                for c in range(tracer_count):
                    value = apply(first_flat, k, g, c, weights, sides[n * count + c])
                    second[c * levels + k, pl.ds(PADR + 8 * g, 8), :] = value
                    done.append(value)
            return acc, tuple(done), ahead

        start = (blank,) * (tracer_count * len(parts[part]))
        acc, done, _ = lax.fori_loop(
            0, levels, level, (start, start, sides_of(part, 0, count)), unroll=2
        )
        return pack(acc, done, levels - 1)

    def second_step(part):
        def level(k, sides):
            ahead = sides_of(part, k + 1, tracer_count)
            for n, g in enumerate(parts[part]):
                weights = [coef[k, w, pl.ds(8 * g, 8), :] for w in range(9)]
                for c in range(tracer_count):
                    final[c * levels + k, pl.ds(8 * g, 8), :] = apply(
                        second_flat, k, g, c, weights, sides[n * tracer_count + c]
                    )
            return ahead

        lax.fori_loop(0, levels, level, sides_of(part, 0, tracer_count), unroll=2)

    fill_rows(first_flat, 0)
    pl.semaphore_wait(barrier, n_dev - 1)
    start_rows(0)
    packed = lax.fori_loop(0, levels, gather_columns, (blank,) * ((tracer_count + 1) * groups), unroll=2)
    packed = [packed[g * (tracer_count + 1) : (g + 1) * (tracer_count + 1)] for g in range(groups)]
    for part in range(2):
        fill_columns(sum([packed[g] for g in parts[part]], ()), 0, part)
        start_columns(0, part)

    for load in loads[4:]:
        load.wait()
    cell_row, owner_row = cell[...], owner[...]
    f_row = lax.broadcasted_iota(jnp.int32, (floats, floats), 0)
    f_col = lax.broadcasted_iota(jnp.int32, (floats, floats), 1)
    diagonal = f_row == f_col
    owner_f = owner_row.astype(jnp.float32)
    owner_col = jnp.sum(jnp.where(diagonal, owner_f, 0.0), axis=1, keepdims=True)
    cell_col = jnp.sum(jnp.where(diagonal, cell_row.astype(jnp.float32), 0.0), axis=1, keepdims=True)
    rank = jnp.sum(
        jnp.where((owner_col == owner_f) & (f_col < f_row), 1.0, 0.0), axis=1, keepdims=True
    )
    slot_col = owner_col * float(BOX) + rank
    slot_lane = lax.broadcasted_iota(jnp.int32, (floats, slots), 1).astype(jnp.float32)
    wanted = jnp.sum(jnp.where(slot_col == slot_lane, cell_col + 1.0, 0.0), axis=0, keepdims=True) - 1.0
    wanted = wanted.astype(jnp.int32)
    slot_row = lax.broadcasted_iota(jnp.int32, (slots, floats), 0)
    tally = jnp.sum(
        jnp.where(owner_row * BOX + CAP == slot_row, 1.0, 0.0), axis=1, keepdims=True
    )

    def mark(r, carry):
        start = pl.multiple_of(r * 128, 128)
        place = lax.broadcasted_iota(jnp.int32, (128, slots), 0) + start
        pick[pl.ds(start, 128), :] = jnp.where(place == wanted, 1.0, 0.0).astype(jnp.bfloat16)
        return carry

    taken[...] = jnp.zeros_like(taken)
    lax.fori_loop(0, rows, mark, 0)

    wait_columns(0, 0)
    place_columns(0, 0)
    packed = first_step(0)
    fill_columns(packed, 1, 0)
    start_columns(1, 0)
    wait_rows(0)
    place_rows(first_flat, 0)
    wait_columns(0, 1)
    place_columns(0, 1)
    packed = first_step(1)
    fill_rows(second_flat, 1)
    start_rows(1)
    fill_columns(packed, 1, 1)
    start_columns(1, 1)

    flat = final.reshape(planes * rows, 128)

    def take(part):
        half = rows // 8

        def four_rows(i, carry):
            start = 4 * (half // 2 + i) if part == 0 else 4 * jnp.where(i < half // 2, i, i + half)
            for j in range(4):
                value = flat[pl.ds(start + j, planes, stride=rows), :]
                high = value.astype(jnp.bfloat16)
                rest = (value - high.astype(jnp.float32)).astype(jnp.bfloat16)
                halves[pl.ds(0, planes), pl.ds(j * 128, 128)] = high
                halves[pl.ds(planes, planes), pl.ds(j * 128, 128)] = rest
            chosen = pick[pl.ds(pl.multiple_of(start * 128, 512), 512), :]
            taken[...] += jnp.dot(halves[...], chosen, preferred_element_type=jnp.float32)
            return carry

        lax.fori_loop(0, half, four_rows, 0)

    wait_columns(1, 0)
    place_columns(1, 0)
    second_step(0)
    take(0)
    wait_rows(1)
    place_rows(second_flat, 1)
    wait_columns(1, 1)
    place_columns(1, 1)
    second_step(1)
    take(1)
    outbox[...] = jnp.transpose(taken[pl.ds(0, planes), :] + taken[pl.ds(planes, planes), :]) + tally

    def box_copy(j):
        other = lax.rem(me + j, n_dev)
        return pltpu.make_async_remote_copy(
            src_ref=outbox.at[pl.ds(pl.multiple_of(other * BOX, BOX), BOX)],
            dst_ref=inbox.at[pl.ds(pl.multiple_of(me * BOX, BOX), BOX)],
            send_sem=box_send.at[other],
            recv_sem=box_recv.at[me],
            device_id=(other // n_lon, lax.rem(other, n_lon)),
            device_id_type=MESH,
        )

    def box_start(j, carry):
        box_copy(j).start()
        return carry

    def box_wait(j, carry):
        other = lax.rem(me + j, n_dev)
        at = pl.ds(pl.multiple_of(other * BOX, BOX), BOX)
        copy = pltpu.make_async_remote_copy(
            src_ref=outbox.at[at],
            dst_ref=inbox.at[at],
            send_sem=box_send.at[other],
            recv_sem=box_recv.at[other],
            device_id=(other // n_lon, lax.rem(other, n_lon)),
            device_id_type=MESH,
        )
        copy.wait()
        return carry

    lax.fori_loop(1, n_dev, box_start, 0)
    own = pl.ds(pl.multiple_of(me * BOX, BOX), BOX)
    inbox[own, :] = outbox[own, :]
    lax.fori_loop(1, n_dev, box_wait, 0)
    for i in range(CAP):
        arrivals[pl.ds(i, n_dev, stride=CAP), :] = inbox[pl.ds(i, n_dev, stride=BOX), :]
    told = inbox[pl.ds(CAP, n_dev, stride=BOX), :][:, :n_dev]
    straight = lax.broadcasted_iota(jnp.int32, (n_dev, n_dev), 0) == lax.broadcasted_iota(
        jnp.int32, (n_dev, n_dev), 1
    )
    counts[...] = jnp.sum(jnp.where(straight, told, 0.0), axis=0, keepdims=True).astype(jnp.int32)


def local(tracers, vel_east, vel_north, land_mask, step_area, float_cell, float_owner):
    tracer_count, levels, rows, columns = tracers.shape
    n_lat, n_lon = lax.axis_size("lat"), lax.axis_size("lon")
    n_dev = n_lat * n_lon
    planes = tracer_count * levels
    tall = rows + 2 * PADR
    floats = float_cell.shape[0]
    row_size = 2 * planes + levels
    col_size = (tracer_count // 2 + 1) * max(rows - 16, 16)
    f32 = jnp.float32
    whole = pl.BlockSpec(memory_space=pl.ANY)
    vmem = pl.BlockSpec(memory_space=pltpu.VMEM)
    out, arrivals, counts = pl.pallas_call(
        functools.partial(kernel, (tracer_count, levels, rows, n_lat, n_lon)),
        out_shape=(
            pltpu.VMEM((planes, rows, columns), f32),
            pltpu.VMEM((n_dev * CAP, planes), f32),
            pltpu.VMEM((1, n_dev), jnp.int32),
        ),
        in_specs=[whole] * 7,
        out_specs=[vmem] * 3,
        scratch_shapes=[
            pltpu.VMEM((rows, columns), f32),
            pltpu.VMEM((1, floats), jnp.int32),
            pltpu.VMEM((1, floats), jnp.int32),
            pltpu.VMEM((levels, rows, columns), jnp.int32),
            pltpu.VMEM((levels, rows, columns), f32),
            pltpu.VMEM((levels, rows, columns), f32),
            pltpu.VMEM((planes, tall, columns), f32),
            pltpu.VMEM((planes, tall, columns), f32),
            pltpu.VMEM((levels, tall, columns), f32),
            pltpu.VMEM((levels, tall, columns), f32),
            pltpu.VMEM((levels, 9, rows, columns), f32),
            pltpu.VMEM((tracer_count + 1, rows, columns), f32),
            *[pltpu.VMEM((2, 2, col_size, columns), f32)] * 4,
            *[pltpu.VMEM((2, row_size, columns), f32)] * 4,
            pltpu.VMEM((rows * columns, n_dev * BOX), jnp.bfloat16),
            pltpu.VMEM((2 * planes, 4 * columns), jnp.bfloat16),
            pltpu.VMEM((2 * planes, n_dev * BOX), f32),
            pltpu.VMEM((n_dev * BOX, planes), f32),
            pltpu.VMEM((n_dev * BOX, planes), f32),
            pltpu.SemaphoreType.DMA((7,)),
            pltpu.SemaphoreType.DMA((2, 6)),
            pltpu.SemaphoreType.DMA((2, 6)),
            pltpu.SemaphoreType.DMA((n_dev,)),
            pltpu.SemaphoreType.DMA((n_dev,)),
        ],
        compiler_params=pltpu.CompilerParams(
            collective_id=0, has_side_effects=True, vmem_limit_bytes=56 * 1024 * 1024
        ),
        cost_estimate=pl.CostEstimate(
            flops=2 * 17 * planes * rows * columns, bytes_accessed=8 * 1024 * 1024, transcendentals=0
        ),
    )(
        step_area,
        float_cell.reshape(1, floats),
        float_owner.reshape(1, floats),
        land_mask,
        vel_east,
        vel_north,
        tracers.reshape(planes, rows, columns),
    )
    return out.reshape(tracers.shape), arrivals, counts.reshape(n_dev)


def solution(mesh):
    placed = (
        P(None, None, "lat", "lon"),
        P(None, "lat", "lon"),
        P(None, "lat", "lon"),
        P(None, "lat", "lon"),
        P("lat", "lon"),
        P(("lat", "lon")),
        P(("lat", "lon"), None),
    )
    return jax.shard_map(
        local,
        mesh=mesh,
        in_specs=placed,
        out_specs=(P(None, None, "lat", "lon"), P(("lat", "lon"), None), P(("lat", "lon"))),
        check_vma=False,
    )
```

```python
import functools

import jax
import jax.numpy as jnp
from jax import lax
from jax.experimental import pallas as pl
from jax.experimental.pallas import tpu as pltpu
from jax.sharding import PartitionSpec as P

CAP = 4
BOX = 8
PADR = 8
MESH = pl.DeviceIdType.MESH


def kernel(
    dims, area_h, cell_h, owner_h, mask_h, east_h, north_h, tracers_h, final, arrivals, counts,
    area, cell, owner, mask, east, north, first, second, wet, flow, coef,
    cols, send_l, send_r, get_l, get_r, send_n, send_s, get_n, get_s,
    pick, halves, taken, outbox, inbox,
    in_sem, halo_send, halo_recv, box_send, box_recv,
):
    tracer_count, levels, rows, n_lat, n_lon = dims
    planes = tracer_count * levels
    tall = rows + 2 * PADR
    n_dev = n_lat * n_lon
    slots = n_dev * BOX
    floats = cell.shape[1]
    lat, lon = lax.axis_index("lat"), lax.axis_index("lon")
    me = lat * n_lon + lon
    top = lat == n_lat - 1
    bottom = lat == 0

    loads = [
        pltpu.make_async_copy(mask_h, mask, in_sem.at[0]),
        pltpu.make_async_copy(east_h, east, in_sem.at[1]),
        pltpu.make_async_copy(north_h, north, in_sem.at[2]),
        pltpu.make_async_copy(tracers_h, first.at[:, pl.ds(PADR, rows), :], in_sem.at[3]),
        pltpu.make_async_copy(area_h, area, in_sem.at[4]),
        pltpu.make_async_copy(cell_h, cell, in_sem.at[5]),
        pltpu.make_async_copy(owner_h, owner, in_sem.at[6]),
    ]
    for load in loads:
        load.start()

    barrier = pltpu.get_barrier_semaphore()

    def greet(j, carry):
        other = lax.rem(me + j, n_dev)
        pl.semaphore_signal(
            barrier, inc=1, device_id=(other // n_lon, lax.rem(other, n_lon)), device_id_type=MESH
        )
        return carry

    lax.fori_loop(1, n_dev, greet, 0)

    lane = lax.broadcasted_iota(jnp.int32, (8, 128), 1)
    group = lane // 4
    low_pair = lax.rem(lane, 4) < 2
    groups = rows // 8

    inner, outer = tuple(range(1, groups - 1)), (0, groups - 1)
    parts = (inner, outer)
    pairs = tracer_count // 2
    first_flat = first.reshape(planes * tall, 128)
    second_flat = second.reshape(planes * tall, 128)
    wet_flat = wet.reshape(levels * tall, 128)
    flow_flat = flow.reshape(levels * tall, 128)
    blank = jnp.zeros((8, 128), jnp.float32)

    for load in loads[:4]:
        load.wait()

    def gather_columns(k, acc):
        acc = list(acc)
        here = group == k
        for g in range(groups):
            at = pl.ds(PADR + 8 * g, 8)
            sub = pl.ds(8 * g, 8)
            water = mask[k, sub, :].astype(jnp.float32)
            wet[k, at, :] = water
            flow[k, at, :] = north[k, sub, :] * water
            edge = jnp.where(lane == 0, water, east[k, sub, :] * water)
            values = [first[c * levels + k, at, :] for c in range(tracer_count)] + [edge]
            for c, value in enumerate(values):
                i = g * (tracer_count + 1) + c
                acc[i] = jnp.where(here, pltpu.roll(value, 4 * k + 2, 1), acc[i])
        return tuple(acc)

    def fill_columns(packed, step, part):
        per = len(packed) // len(parts[part])
        for n in range(len(parts[part])):
            mine = packed[n * per : (n + 1) * per]
            for pair in range(pairs):
                a, b = mine[2 * pair], mine[2 * pair + 1]
                sub = pl.ds(pair * 8 * len(parts[part]) + 8 * n, 8)
                send_r[step, part, sub, :] = jnp.where(low_pair, a, pltpu.roll(b, 2, 1))
                send_l[step, part, sub, :] = jnp.where(low_pair, pltpu.roll(b, 126, 1), a)
            if step == 0:
                sub = pl.ds(pairs * 8 * len(parts[part]) + 8 * n, 8)
                send_r[step, part, sub, :] = mine[tracer_count]
                send_l[step, part, sub, :] = mine[tracer_count]

    def place_columns(step, part):
        for n, g in enumerate(parts[part]):
            at = pl.ds(8 * g, 8)
            for pair in range(pairs):
                sub = pl.ds(pair * 8 * len(parts[part]) + 8 * n, 8)
                from_l, from_r = get_l[step, part, sub, :], get_r[step, part, sub, :]
                cols[2 * pair, at, :] = jnp.where(low_pair, from_l, from_r)
                cols[2 * pair + 1, at, :] = jnp.where(
                    low_pair, pltpu.roll(from_l, 126, 1), pltpu.roll(from_r, 2, 1)
                )
            if step == 0:
                sub = pl.ds(pairs * 8 * len(parts[part]) + 8 * n, 8)
                cols[tracer_count, at, :] = jnp.where(
                    low_pair, get_l[step, part, sub, :], get_r[step, part, sub, :]
                )

    def fill_rows(flat, step):
        def row(r):
            return flat[pl.ds(PADR + r, planes, stride=tall), :]

        def water(r):
            line = mask.reshape(levels * rows, 128)[pl.ds(r, levels, stride=rows), :]
            return line.astype(jnp.float32)

        def stream(r):
            return north.reshape(levels * rows, 128)[pl.ds(r, levels, stride=rows), :] * water(r)

        last, before = row(rows - 1), row(rows - 2)
        send_n[step, pl.ds(0, planes), :] = jnp.where(top, last, before)
        send_n[step, pl.ds(planes, planes), :] = jnp.where(top, before, last)
        if step == 0:
            send_n[step, pl.ds(2 * planes, levels), :] = jnp.where(
                top, water(rows - 1), stream(rows - 1)
            )

        @pl.when(top)
        def _():
            ahead = lax.rem(lax.broadcasted_iota(jnp.int32, (256, 128), 0), 128)
            across = lax.broadcasted_iota(jnp.int32, (256, 128), 1)
            turn = jnp.where(ahead + across == 127, 1.0, 0.0).astype(jnp.bfloat16)

            def reverse(at):
                value = send_n[step, at, :]
                high = value.astype(jnp.bfloat16)
                rest = (value - high.astype(jnp.float32)).astype(jnp.bfloat16)
                send_n[step, at, :] = jnp.dot(
                    jnp.concatenate([high, rest], axis=1), turn, preferred_element_type=jnp.float32
                )

            reverse(pl.ds(0, 2 * planes))
            if step == 0:
                reverse(pl.ds(2 * planes, levels))

        send_s[step, pl.ds(0, planes), :] = row(0)
        send_s[step, pl.ds(planes, planes), :] = row(1)
        if step == 0:
            send_s[step, pl.ds(2 * planes, levels), :] = water(0)

    right, left = lax.rem(lon + 1, n_lon), lax.rem(lon + n_lon - 1, n_lon)
    upper = (jnp.where(top, lat, lat + 1), jnp.where(top, n_lon - 1 - lon, lon))
    lower = (jnp.where(bottom, 0, lat - 1), lon)

    def column_copies(step, part):
        size = (pairs + (1 if step == 0 else 0)) * 8 * len(parts[part])
        return [
            pltpu.make_async_remote_copy(
                src_ref=source.at[step, part, pl.ds(0, size)],
                dst_ref=target.at[step, part, pl.ds(0, size)],
                send_sem=halo_send.at[step, 2 * part + i],
                recv_sem=halo_recv.at[step, 2 * part + i],
                device_id=(lat, device),
                device_id_type=MESH,
            )
            for i, (source, target, device) in enumerate(
                ((send_r, get_l, right), (send_l, get_r, left))
            )
        ]

    def start_columns(step, part):
        for copy in column_copies(step, part):
            copy.start()

    def wait_columns(step, part):
        for copy in column_copies(step, part):
            copy.wait()

    def row_copy(step, source, target, out, come, device):
        size = 2 * planes + (levels if step == 0 else 0)
        return pltpu.make_async_remote_copy(
            src_ref=source.at[step, pl.ds(0, size)],
            dst_ref=target.at[step, pl.ds(0, size)],
            send_sem=halo_send.at[step, out],
            recv_sem=halo_recv.at[step, come],
            device_id=device,
            device_id_type=MESH,
        )

    def up_copy(step):
        return row_copy(step, send_n, get_s, 4, 4, upper)

    def down_copy(step):
        return row_copy(step, send_s, get_n, 5, 5, lower)

    def fold_copy(step):
        return row_copy(step, send_n, get_n, 4, 5, upper)

    def start_rows(step):
        @pl.when(top)
        def _():
            fold_copy(step).start()

        @pl.when(jnp.logical_not(top))
        def _():
            up_copy(step).start()

        @pl.when(jnp.logical_not(bottom))
        def _():
            down_copy(step).start()

    def wait_rows(step):
        up_copy(step).wait_send()
        down_copy(step).wait_recv()

        @pl.when(jnp.logical_not(bottom))
        def _():
            down_copy(step).wait_send()
            up_copy(step).wait_recv()

    def place_rows(flat, step):
        for i in range(2):
            flat[pl.ds(PADR + rows + i, planes, stride=tall), :] = get_n[
                step, pl.ds(i * planes, planes), :
            ]
        if step == 0:
            wet_flat[pl.ds(PADR + rows, levels, stride=tall), :] = get_n[
                step, pl.ds(2 * planes, levels), :
            ]

        @pl.when(bottom)
        def _():
            for i in range(2):
                flat[pl.ds(PADR - 2 + i, planes, stride=tall), :] = jnp.zeros((planes, 128), jnp.float32)
            if step == 0:
                flow_flat[pl.ds(PADR - 1, levels, stride=tall), :] = jnp.zeros((levels, 128), jnp.float32)

        @pl.when(jnp.logical_not(bottom))
        def _():
            for i in range(2):
                flat[pl.ds(PADR - 2 + i, planes, stride=tall), :] = get_s[
                    step, pl.ds(i * planes, planes), :
                ]
            if step == 0:
                flow_flat[pl.ds(PADR - 1, levels, stride=tall), :] = get_s[
                    step, pl.ds(2 * planes, levels), :
                ]

    def make_coefficients(k, g, beside):
        at = pl.ds(PADR + 8 * g, 8)
        sub = pl.ds(8 * g, 8)
        water = wet[k, at, :]
        scale = area[sub, :] * water * (1.0 / 6.0)
        stream = east[k, sub, :] * water
        face_e = stream * pltpu.roll(jnp.where(lane == 0, beside, water), 127, 1)
        face_w = pltpu.roll(jnp.where(lane == 127, beside, stream), 1, 1) * water
        line = k * tall + PADR + 8 * g
        face_n = flow[k, at, :] * wet_flat[pl.ds(line + 1, 8), :]
        face_s = flow_flat[pl.ds(line - 1, 8), :] * water
        made = []
        centre = 1.0
        for ahead, behind in ((face_e, face_w), (face_n, face_s)):
            pos, neg = jnp.maximum(ahead, 0.0) * scale, jnp.minimum(ahead, 0.0) * scale
            pos_b, neg_b = jnp.maximum(behind, 0.0) * scale, jnp.minimum(behind, 0.0) * scale
            centre = centre - (5.0 * (pos - neg_b) + 2.0 * (neg - pos_b))
            made += [
                -pos_b,
                pos + 5.0 * pos_b + 2.0 * neg_b,
                -(2.0 * pos + 5.0 * neg + neg_b),
                neg,
            ]
        return [centre] + made

    def sides_of(part, k, count):
        shift = (126 - 4 * k) & 127
        return tuple(
            pltpu.roll(cols[c, pl.ds(8 * g, 8), :], shift, 1) for g in parts[part] for c in range(count)
        )

    def apply(flat, k, g, c, weights, beside):
        centre, xm2, xm1, xp1, xp2, ym2, ym1, yp1, yp2 = weights
        base = (c * levels + k) * tall + PADR + 8 * g
        value = flat[pl.ds(pl.multiple_of(base, 8), 8), :]
        total = centre * value
        total += ym2 * flat[pl.ds(base - 2, 8), :]
        total += ym1 * flat[pl.ds(base - 1, 8), :]
        total += yp1 * flat[pl.ds(base + 1, 8), :]
        total += yp2 * flat[pl.ds(base + 2, 8), :]
        total += xm2 * pltpu.roll(jnp.where(lane >= 126, beside, value), 2, 1)
        total += xm1 * pltpu.roll(jnp.where(lane == 127, beside, value), 1, 1)
        total += xp1 * pltpu.roll(jnp.where(lane == 0, beside, value), 127, 1)
        total += xp2 * pltpu.roll(jnp.where(lane <= 1, beside, value), 126, 1)
        return total

    def first_step(part):
        count = tracer_count + 1

        def pack(acc, done, k):
            here = group == k
            shift = (4 * k + 2) & 127
            return tuple(jnp.where(here, pltpu.roll(v, shift, 1), a) for a, v in zip(acc, done))

        def level(k, carry):
            acc, done, sides = carry
            acc = pack(acc, done, k - 1)
            ahead = sides_of(part, k + 1, count)
            done = []
            for n, g in enumerate(parts[part]):
                weights = make_coefficients(k, g, sides[n * count + tracer_count])
                for w, weight in enumerate(weights):
                    coef[k, w, pl.ds(8 * g, 8), :] = weight
                for c in range(tracer_count):
                    value = apply(first_flat, k, g, c, weights, sides[n * count + c])
                    second[c * levels + k, pl.ds(PADR + 8 * g, 8), :] = value
                    done.append(value)
            return acc, tuple(done), ahead

        start = (blank,) * (tracer_count * len(parts[part]))
        acc, done, _ = lax.fori_loop(
            0, levels, level, (start, start, sides_of(part, 0, count)), unroll=4
        )
        return pack(acc, done, levels - 1)

    def second_step(part):
        def level(k, sides):
            ahead = sides_of(part, k + 1, tracer_count)
            for n, g in enumerate(parts[part]):
                weights = [coef[k, w, pl.ds(8 * g, 8), :] for w in range(9)]
                for c in range(tracer_count):
                    final[c * levels + k, pl.ds(8 * g, 8), :] = apply(
                        second_flat, k, g, c, weights, sides[n * tracer_count + c]
                    )
            return ahead

        lax.fori_loop(0, levels, level, sides_of(part, 0, tracer_count), unroll=4)

    fill_rows(first_flat, 0)
    pl.semaphore_wait(barrier, n_dev - 1)
    start_rows(0)
    packed = lax.fori_loop(0, levels, gather_columns, (blank,) * ((tracer_count + 1) * groups), unroll=2)
    packed = [packed[g * (tracer_count + 1) : (g + 1) * (tracer_count + 1)] for g in range(groups)]
    for part in range(2):
        fill_columns(sum([packed[g] for g in parts[part]], ()), 0, part)
        start_columns(0, part)

    for load in loads[4:]:
        load.wait()
    cell_row, owner_row = cell[...], owner[...]
    f_row = lax.broadcasted_iota(jnp.int32, (floats, floats), 0)
    f_col = lax.broadcasted_iota(jnp.int32, (floats, floats), 1)
    diagonal = f_row == f_col
    owner_f = owner_row.astype(jnp.float32)
    owner_col = jnp.sum(jnp.where(diagonal, owner_f, 0.0), axis=1, keepdims=True)
    cell_col = jnp.sum(jnp.where(diagonal, cell_row.astype(jnp.float32), 0.0), axis=1, keepdims=True)
    rank = jnp.sum(
        jnp.where((owner_col == owner_f) & (f_col < f_row), 1.0, 0.0), axis=1, keepdims=True
    )
    slot_col = owner_col * float(BOX) + rank
    slot_lane = lax.broadcasted_iota(jnp.int32, (floats, slots), 1).astype(jnp.float32)
    wanted = jnp.sum(jnp.where(slot_col == slot_lane, cell_col + 1.0, 0.0), axis=0, keepdims=True) - 1.0
    wanted = wanted.astype(jnp.int32)
    slot_row = lax.broadcasted_iota(jnp.int32, (slots, floats), 0)
    tally = jnp.sum(
        jnp.where(owner_row * BOX + CAP == slot_row, 1.0, 0.0), axis=1, keepdims=True
    )

    def mark(r, carry):
        start = pl.multiple_of(r * 128, 128)
        place = lax.broadcasted_iota(jnp.int32, (128, slots), 0) + start
        pick[pl.ds(start, 128), :] = jnp.where(place == wanted, 1.0, 0.0).astype(jnp.bfloat16)
        return carry

    taken[...] = jnp.zeros_like(taken)
    lax.fori_loop(0, rows, mark, 0)

    wait_columns(0, 0)
    place_columns(0, 0)
    packed = first_step(0)
    fill_columns(packed, 1, 0)
    start_columns(1, 0)
    wait_rows(0)
    place_rows(first_flat, 0)
    wait_columns(0, 1)
    place_columns(0, 1)
    packed = first_step(1)
    fill_rows(second_flat, 1)
    start_rows(1)
    fill_columns(packed, 1, 1)
    start_columns(1, 1)

    flat = final.reshape(planes * rows, 128)

    def take(part):
        half = rows // 8

        def four_rows(i, carry):
            start = 4 * (half // 2 + i) if part == 0 else 4 * jnp.where(i < half // 2, i, i + half)
            for j in range(4):
                value = flat[pl.ds(start + j, planes, stride=rows), :]
                high = value.astype(jnp.bfloat16)
                rest = (value - high.astype(jnp.float32)).astype(jnp.bfloat16)
                halves[pl.ds(0, planes), pl.ds(j * 128, 128)] = high
                halves[pl.ds(planes, planes), pl.ds(j * 128, 128)] = rest
            chosen = pick[pl.ds(pl.multiple_of(start * 128, 512), 512), :]
            taken[...] += jnp.dot(halves[...], chosen, preferred_element_type=jnp.float32)
            return carry

        lax.fori_loop(0, half, four_rows, 0)

    wait_columns(1, 0)
    place_columns(1, 0)
    second_step(0)
    take(0)
    wait_rows(1)
    place_rows(second_flat, 1)
    wait_columns(1, 1)
    place_columns(1, 1)
    second_step(1)
    take(1)
    outbox[...] = jnp.transpose(taken[pl.ds(0, planes), :] + taken[pl.ds(planes, planes), :]) + tally

    own = pl.ds(pl.multiple_of(me * BOX, BOX), BOX)

    def after_me(j):
        return jnp.where(me + j >= n_dev, me + j - n_dev, me + j)

    def box_start(j, carry):
        other = after_me(j)
        pltpu.make_async_remote_copy(
            src_ref=outbox.at[pl.ds(pl.multiple_of(other * BOX, BOX), BOX)],
            dst_ref=inbox.at[own],
            send_sem=box_send.at[0],
            recv_sem=box_recv.at[0],
            device_id=(lax.div(other, n_lon), lax.rem(other, n_lon)),
            device_id_type=MESH,
        ).start()
        return carry

    lax.fori_loop(1, n_dev, box_start, 0)
    others = pl.ds(0, (n_dev - 1) * BOX)
    pltpu.make_async_remote_copy(
        src_ref=outbox.at[others],
        dst_ref=inbox.at[others],
        send_sem=box_send.at[0],
        recv_sem=box_recv.at[0],
        device_id=(lat, right),
        device_id_type=MESH,
    ).wait()
    inbox[own, :] = outbox[own, :]
    for i in range(CAP):
        arrivals[pl.ds(i, n_dev, stride=CAP), :] = inbox[pl.ds(i, n_dev, stride=BOX), :]
    told = inbox[pl.ds(CAP, n_dev, stride=BOX), :][:, :n_dev]
    straight = lax.broadcasted_iota(jnp.int32, (n_dev, n_dev), 0) == lax.broadcasted_iota(
        jnp.int32, (n_dev, n_dev), 1
    )
    counts[...] = jnp.sum(jnp.where(straight, told, 0.0), axis=0, keepdims=True).astype(jnp.int32)


def local(tracers, vel_east, vel_north, land_mask, step_area, float_cell, float_owner):
    tracer_count, levels, rows, columns = tracers.shape
    n_lat, n_lon = lax.axis_size("lat"), lax.axis_size("lon")
    n_dev = n_lat * n_lon
    planes = tracer_count * levels
    tall = rows + 2 * PADR
    floats = float_cell.shape[0]
    row_size = 2 * planes + levels
    col_size = (tracer_count // 2 + 1) * max(rows - 16, 16)
    f32 = jnp.float32
    whole = pl.BlockSpec(memory_space=pl.ANY)
    vmem = pl.BlockSpec(memory_space=pltpu.VMEM)
    out, arrivals, counts = pl.pallas_call(
        functools.partial(kernel, (tracer_count, levels, rows, n_lat, n_lon)),
        out_shape=(
            pltpu.VMEM((planes, rows, columns), f32),
            pltpu.VMEM((n_dev * CAP, planes), f32),
            pltpu.VMEM((1, n_dev), jnp.int32),
        ),
        in_specs=[whole] * 7,
        out_specs=[vmem] * 3,
        scratch_shapes=[
            pltpu.VMEM((rows, columns), f32),
            pltpu.VMEM((1, floats), jnp.int32),
            pltpu.VMEM((1, floats), jnp.int32),
            pltpu.VMEM((levels, rows, columns), jnp.int32),
            pltpu.VMEM((levels, rows, columns), f32),
            pltpu.VMEM((levels, rows, columns), f32),
            pltpu.VMEM((planes, tall, columns), f32),
            pltpu.VMEM((planes, tall, columns), f32),
            pltpu.VMEM((levels, tall, columns), f32),
            pltpu.VMEM((levels, tall, columns), f32),
            pltpu.VMEM((levels, 9, rows, columns), f32),
            pltpu.VMEM((tracer_count + 1, rows, columns), f32),
            *[pltpu.VMEM((2, 2, col_size, columns), f32)] * 4,
            *[pltpu.VMEM((2, row_size, columns), f32)] * 4,
            pltpu.VMEM((rows * columns, n_dev * BOX), jnp.bfloat16),
            pltpu.VMEM((2 * planes, 4 * columns), jnp.bfloat16),
            pltpu.VMEM((2 * planes, n_dev * BOX), f32),
            pltpu.VMEM((n_dev * BOX, planes), f32),
            pltpu.VMEM((n_dev * BOX, planes), f32),
            pltpu.SemaphoreType.DMA((7,)),
            pltpu.SemaphoreType.DMA((2, 6)),
            pltpu.SemaphoreType.DMA((2, 6)),
            pltpu.SemaphoreType.DMA((1,)),
            pltpu.SemaphoreType.DMA((1,)),
        ],
        compiler_params=pltpu.CompilerParams(
            collective_id=0, has_side_effects=True, vmem_limit_bytes=56 * 1024 * 1024
        ),
        cost_estimate=pl.CostEstimate(
            flops=2 * 17 * planes * rows * columns, bytes_accessed=8 * 1024 * 1024, transcendentals=0
        ),
    )(
        step_area,
        float_cell.reshape(1, floats),
        float_owner.reshape(1, floats),
        land_mask,
        vel_east,
        vel_north,
        tracers.reshape(planes, rows, columns),
    )
    return out.reshape(tracers.shape), arrivals, counts.reshape(n_dev)


def solution(mesh):
    placed = (
        P(None, None, "lat", "lon"),
        P(None, "lat", "lon"),
        P(None, "lat", "lon"),
        P(None, "lat", "lon"),
        P("lat", "lon"),
        P(("lat", "lon")),
        P(("lat", "lon"), None),
    )
    return jax.shard_map(
        local,
        mesh=mesh,
        in_specs=placed,
        out_specs=(P(None, None, "lat", "lon"), P(("lat", "lon"), None), P(("lat", "lon"))),
        check_vma=False,
    )
```

```python
import functools

import jax
import jax.numpy as jnp
from jax import lax
from jax.experimental import pallas as pl
from jax.experimental.pallas import tpu as pltpu
from jax.sharding import PartitionSpec as P

CAP = 4
BOX = 8
PADR = 8
MESH = pl.DeviceIdType.MESH


def kernel(
    dims, area_h, cell_h, owner_h, mask_h, east_h, north_h, tracers_h, final, arrivals, counts,
    area, cell, owner, mask, east, north, first, second, wet, flow, coef,
    cols, send_l, send_r, get_l, get_r, send_n, send_s, get_n, get_s,
    pick, halves, taken, outbox, inbox,
    in_sem, halo_send, halo_recv, box_send, box_recv,
):
    tracer_count, levels, rows, n_lat, n_lon = dims
    planes = tracer_count * levels
    tall = rows + 2 * PADR
    n_dev = n_lat * n_lon
    slots = n_dev * BOX
    floats = cell.shape[1]
    lat, lon = lax.axis_index("lat"), lax.axis_index("lon")
    me = lat * n_lon + lon
    top = lat == n_lat - 1
    bottom = lat == 0

    loads = [
        pltpu.make_async_copy(mask_h, mask, in_sem.at[0]),
        pltpu.make_async_copy(east_h, east, in_sem.at[1]),
        pltpu.make_async_copy(north_h, north, in_sem.at[2]),
        pltpu.make_async_copy(tracers_h, first.at[:, pl.ds(PADR, rows), :], in_sem.at[3]),
        pltpu.make_async_copy(area_h, area, in_sem.at[4]),
        pltpu.make_async_copy(cell_h, cell, in_sem.at[5]),
        pltpu.make_async_copy(owner_h, owner, in_sem.at[6]),
    ]
    for load in loads:
        load.start()

    barrier = pltpu.get_barrier_semaphore()

    def after_me(j):
        return jnp.where(me + j >= n_dev, me + j - n_dev, me + j)

    def greet(j, carry):
        other = after_me(j)
        pl.semaphore_signal(
            barrier,
            inc=1,
            device_id=(lax.div(other, n_lon), lax.rem(other, n_lon)),
            device_id_type=MESH,
        )
        return carry

    lax.fori_loop(1, n_dev, greet, 0)

    lane = lax.broadcasted_iota(jnp.int32, (8, 128), 1)
    group = lane // 4
    low_pair = lax.rem(lane, 4) < 2
    groups = rows // 8

    inner, outer = tuple(range(1, groups - 1)), (0, groups - 1)
    parts = (inner, outer)
    pairs = tracer_count // 2
    first_flat = first.reshape(planes * tall, 128)
    second_flat = second.reshape(planes * tall, 128)
    wet_flat = wet.reshape(levels * tall, 128)
    flow_flat = flow.reshape(levels * tall, 128)
    blank = jnp.zeros((8, 128), jnp.float32)

    for load in loads[:4]:
        load.wait()

    def gather_columns(k, acc):
        acc = list(acc)
        here = group == k
        for g in range(groups):
            at = pl.ds(PADR + 8 * g, 8)
            sub = pl.ds(8 * g, 8)
            water = mask[k, sub, :].astype(jnp.float32)
            wet[k, at, :] = water
            flow[k, at, :] = north[k, sub, :] * water
            edge = jnp.where(lane == 0, water, east[k, sub, :] * water)
            values = [first[c * levels + k, at, :] for c in range(tracer_count)] + [edge]
            for c, value in enumerate(values):
                i = g * (tracer_count + 1) + c
                acc[i] = jnp.where(here, pltpu.roll(value, 4 * k + 2, 1), acc[i])
        return tuple(acc)

    def fill_columns(packed, step, part):
        per = len(packed) // len(parts[part])
        for n in range(len(parts[part])):
            mine = packed[n * per : (n + 1) * per]
            for pair in range(pairs):
                a, b = mine[2 * pair], mine[2 * pair + 1]
                sub = pl.ds(pair * 8 * len(parts[part]) + 8 * n, 8)
                send_r[step, part, sub, :] = jnp.where(low_pair, a, pltpu.roll(b, 2, 1))
                send_l[step, part, sub, :] = jnp.where(low_pair, pltpu.roll(b, 126, 1), a)
            if step == 0:
                sub = pl.ds(pairs * 8 * len(parts[part]) + 8 * n, 8)
                send_r[step, part, sub, :] = mine[tracer_count]
                send_l[step, part, sub, :] = mine[tracer_count]

    def place_columns(step, part):
        for n, g in enumerate(parts[part]):
            at = pl.ds(8 * g, 8)
            for pair in range(pairs):
                sub = pl.ds(pair * 8 * len(parts[part]) + 8 * n, 8)
                from_l, from_r = get_l[step, part, sub, :], get_r[step, part, sub, :]
                cols[2 * pair, at, :] = jnp.where(low_pair, from_l, from_r)
                cols[2 * pair + 1, at, :] = jnp.where(
                    low_pair, pltpu.roll(from_l, 126, 1), pltpu.roll(from_r, 2, 1)
                )
            if step == 0:
                sub = pl.ds(pairs * 8 * len(parts[part]) + 8 * n, 8)
                cols[tracer_count, at, :] = jnp.where(
                    low_pair, get_l[step, part, sub, :], get_r[step, part, sub, :]
                )

    def fill_rows(flat, step):
        def row(r):
            return flat[pl.ds(PADR + r, planes, stride=tall), :]

        def water(r):
            line = mask.reshape(levels * rows, 128)[pl.ds(r, levels, stride=rows), :]
            return line.astype(jnp.float32)

        def stream(r):
            return north.reshape(levels * rows, 128)[pl.ds(r, levels, stride=rows), :] * water(r)

        last, before = row(rows - 1), row(rows - 2)
        send_n[step, pl.ds(0, planes), :] = jnp.where(top, last, before)
        send_n[step, pl.ds(planes, planes), :] = jnp.where(top, before, last)
        if step == 0:
            send_n[step, pl.ds(2 * planes, levels), :] = jnp.where(
                top, water(rows - 1), stream(rows - 1)
            )

        @pl.when(top)
        def _():
            ahead = lax.rem(lax.broadcasted_iota(jnp.int32, (256, 128), 0), 128)
            across = lax.broadcasted_iota(jnp.int32, (256, 128), 1)
            turn = jnp.where(ahead + across == 127, 1.0, 0.0).astype(jnp.bfloat16)

            def reverse(at):
                value = send_n[step, at, :]
                high = value.astype(jnp.bfloat16)
                rest = (value - high.astype(jnp.float32)).astype(jnp.bfloat16)
                send_n[step, at, :] = jnp.dot(
                    jnp.concatenate([high, rest], axis=1), turn, preferred_element_type=jnp.float32
                )

            reverse(pl.ds(0, 2 * planes))
            if step == 0:
                reverse(pl.ds(2 * planes, levels))

        send_s[step, pl.ds(0, planes), :] = row(0)
        send_s[step, pl.ds(planes, planes), :] = row(1)
        if step == 0:
            send_s[step, pl.ds(2 * planes, levels), :] = water(0)

    right, left = lax.rem(lon + 1, n_lon), lax.rem(lon + n_lon - 1, n_lon)
    upper = (jnp.where(top, lat, lat + 1), jnp.where(top, n_lon - 1 - lon, lon))
    lower = (jnp.where(bottom, 0, lat - 1), lon)

    def column_copies(step, part):
        size = (pairs + (1 if step == 0 else 0)) * 8 * len(parts[part])
        return [
            pltpu.make_async_remote_copy(
                src_ref=source.at[step, part, pl.ds(0, size)],
                dst_ref=target.at[step, part, pl.ds(0, size)],
                send_sem=halo_send.at[step, 2 * part + i],
                recv_sem=halo_recv.at[step, 2 * part + i],
                device_id=(lat, device),
                device_id_type=MESH,
            )
            for i, (source, target, device) in enumerate(
                ((send_r, get_l, right), (send_l, get_r, left))
            )
        ]

    def start_columns(step, part):
        for copy in column_copies(step, part):
            copy.start()

    def wait_columns(step, part):
        for copy in column_copies(step, part):
            copy.wait()

    def row_copy(step, source, target, out, come, device):
        size = 2 * planes + (levels if step == 0 else 0)
        return pltpu.make_async_remote_copy(
            src_ref=source.at[step, pl.ds(0, size)],
            dst_ref=target.at[step, pl.ds(0, size)],
            send_sem=halo_send.at[step, out],
            recv_sem=halo_recv.at[step, come],
            device_id=device,
            device_id_type=MESH,
        )

    def up_copy(step):
        return row_copy(step, send_n, get_s, 4, 4, upper)

    def down_copy(step):
        return row_copy(step, send_s, get_n, 5, 5, lower)

    def fold_copy(step):
        return row_copy(step, send_n, get_n, 4, 5, upper)

    def start_rows(step):
        @pl.when(top)
        def _():
            fold_copy(step).start()

        @pl.when(jnp.logical_not(top))
        def _():
            up_copy(step).start()

        @pl.when(jnp.logical_not(bottom))
        def _():
            down_copy(step).start()

    def wait_rows(step):
        up_copy(step).wait_send()
        down_copy(step).wait_recv()

        @pl.when(jnp.logical_not(bottom))
        def _():
            down_copy(step).wait_send()
            up_copy(step).wait_recv()

    def place_rows(flat, step):
        for i in range(2):
            flat[pl.ds(PADR + rows + i, planes, stride=tall), :] = get_n[
                step, pl.ds(i * planes, planes), :
            ]
        if step == 0:
            wet_flat[pl.ds(PADR + rows, levels, stride=tall), :] = get_n[
                step, pl.ds(2 * planes, levels), :
            ]

        @pl.when(bottom)
        def _():
            for i in range(2):
                flat[pl.ds(PADR - 2 + i, planes, stride=tall), :] = jnp.zeros((planes, 128), jnp.float32)
            if step == 0:
                flow_flat[pl.ds(PADR - 1, levels, stride=tall), :] = jnp.zeros((levels, 128), jnp.float32)

        @pl.when(jnp.logical_not(bottom))
        def _():
            for i in range(2):
                flat[pl.ds(PADR - 2 + i, planes, stride=tall), :] = get_s[
                    step, pl.ds(i * planes, planes), :
                ]
            if step == 0:
                flow_flat[pl.ds(PADR - 1, levels, stride=tall), :] = get_s[
                    step, pl.ds(2 * planes, levels), :
                ]

    def make_coefficients(k, g, beside):
        at = pl.ds(PADR + 8 * g, 8)
        sub = pl.ds(8 * g, 8)
        water = wet[k, at, :]
        scale = area[sub, :] * water * (1.0 / 6.0)
        stream = east[k, sub, :] * water
        face_e = stream * pltpu.roll(jnp.where(lane == 0, beside, water), 127, 1)
        face_w = pltpu.roll(jnp.where(lane == 127, beside, stream), 1, 1) * water
        line = k * tall + PADR + 8 * g
        face_n = flow[k, at, :] * wet_flat[pl.ds(line + 1, 8), :]
        face_s = flow_flat[pl.ds(line - 1, 8), :] * water
        made = []
        centre = 1.0
        for ahead, behind in ((face_e, face_w), (face_n, face_s)):
            pos, neg = jnp.maximum(ahead, 0.0) * scale, jnp.minimum(ahead, 0.0) * scale
            pos_b, neg_b = jnp.maximum(behind, 0.0) * scale, jnp.minimum(behind, 0.0) * scale
            centre = centre - (5.0 * (pos - neg_b) + 2.0 * (neg - pos_b))
            made += [
                -pos_b,
                pos + 5.0 * pos_b + 2.0 * neg_b,
                -(2.0 * pos + 5.0 * neg + neg_b),
                neg,
            ]
        return [centre] + made

    def sides_of(part, k, count):
        shift = (126 - 4 * k) & 127
        return tuple(
            pltpu.roll(cols[c, pl.ds(8 * g, 8), :], shift, 1) for g in parts[part] for c in range(count)
        )

    def apply(flat, k, g, c, weights, beside):
        centre, xm2, xm1, xp1, xp2, ym2, ym1, yp1, yp2 = weights
        base = (c * levels + k) * tall + PADR + 8 * g
        value = flat[pl.ds(pl.multiple_of(base, 8), 8), :]
        total = centre * value
        total += ym2 * flat[pl.ds(base - 2, 8), :]
        total += ym1 * flat[pl.ds(base - 1, 8), :]
        total += yp1 * flat[pl.ds(base + 1, 8), :]
        total += yp2 * flat[pl.ds(base + 2, 8), :]
        total += xm2 * pltpu.roll(jnp.where(lane >= 126, beside, value), 2, 1)
        total += xm1 * pltpu.roll(jnp.where(lane == 127, beside, value), 1, 1)
        total += xp1 * pltpu.roll(jnp.where(lane == 0, beside, value), 127, 1)
        total += xp2 * pltpu.roll(jnp.where(lane <= 1, beside, value), 126, 1)
        return total

    def first_step(part):
        count = tracer_count + 1

        def pack(acc, done, k):
            here = group == k
            shift = (4 * k + 2) & 127
            return tuple(jnp.where(here, pltpu.roll(v, shift, 1), a) for a, v in zip(acc, done))

        def level(k, carry):
            acc, done, sides = carry
            acc = pack(acc, done, k - 1)
            ahead = sides_of(part, k + 1, count)
            done = []
            for n, g in enumerate(parts[part]):
                weights = make_coefficients(k, g, sides[n * count + tracer_count])
                for w, weight in enumerate(weights):
                    coef[k, w, pl.ds(8 * g, 8), :] = weight
                for c in range(tracer_count):
                    value = apply(first_flat, k, g, c, weights, sides[n * count + c])
                    second[c * levels + k, pl.ds(PADR + 8 * g, 8), :] = value
                    done.append(value)
            return acc, tuple(done), ahead

        start = (blank,) * (tracer_count * len(parts[part]))
        acc, done, _ = lax.fori_loop(
            0, levels, level, (start, start, sides_of(part, 0, count)), unroll=4
        )
        return pack(acc, done, levels - 1)

    def second_step(part):
        def level(k, sides):
            ahead = sides_of(part, k + 1, tracer_count)
            for n, g in enumerate(parts[part]):
                weights = [coef[k, w, pl.ds(8 * g, 8), :] for w in range(9)]
                for c in range(tracer_count):
                    final[c * levels + k, pl.ds(8 * g, 8), :] = apply(
                        second_flat, k, g, c, weights, sides[n * tracer_count + c]
                    )
            return ahead

        lax.fori_loop(0, levels, level, sides_of(part, 0, tracer_count), unroll=4)

    fill_rows(first_flat, 0)
    pl.semaphore_wait(barrier, n_dev - 1)
    start_rows(0)
    packed = lax.fori_loop(0, levels, gather_columns, (blank,) * ((tracer_count + 1) * groups), unroll=2)
    packed = [packed[g * (tracer_count + 1) : (g + 1) * (tracer_count + 1)] for g in range(groups)]
    for part in range(2):
        fill_columns(sum([packed[g] for g in parts[part]], ()), 0, part)
        start_columns(0, part)

    for load in loads[4:]:
        load.wait()
    cell_row, owner_row = cell[...], owner[...]
    f_row = lax.broadcasted_iota(jnp.int32, (floats, floats), 0)
    f_col = lax.broadcasted_iota(jnp.int32, (floats, floats), 1)
    diagonal = f_row == f_col
    owner_f = owner_row.astype(jnp.float32)
    owner_col = jnp.sum(jnp.where(diagonal, owner_f, 0.0), axis=1, keepdims=True)
    cell_col = jnp.sum(jnp.where(diagonal, cell_row.astype(jnp.float32), 0.0), axis=1, keepdims=True)
    rank = jnp.sum(
        jnp.where((owner_col == owner_f) & (f_col < f_row), 1.0, 0.0), axis=1, keepdims=True
    )
    slot_col = owner_col * float(BOX) + rank
    slot_lane = lax.broadcasted_iota(jnp.int32, (floats, slots), 1).astype(jnp.float32)
    wanted = jnp.sum(jnp.where(slot_col == slot_lane, cell_col + 1.0, 0.0), axis=0, keepdims=True) - 1.0
    wanted = wanted.astype(jnp.int32)
    slot_row = lax.broadcasted_iota(jnp.int32, (slots, floats), 0)
    tally = jnp.sum(
        jnp.where(owner_row * BOX + CAP == slot_row, 1.0, 0.0), axis=1, keepdims=True
    )

    def mark(r, carry):
        start = pl.multiple_of(r * 128, 128)
        place = lax.broadcasted_iota(jnp.int32, (128, slots), 0) + start
        pick[pl.ds(start, 128), :] = jnp.where(place == wanted, 1.0, 0.0).astype(jnp.bfloat16)
        return carry

    taken[...] = jnp.zeros_like(taken)
    lax.fori_loop(0, rows, mark, 0)

    wait_columns(0, 0)
    place_columns(0, 0)
    packed = first_step(0)
    fill_columns(packed, 1, 0)
    start_columns(1, 0)
    wait_rows(0)
    place_rows(first_flat, 0)
    wait_columns(0, 1)
    place_columns(0, 1)
    packed = first_step(1)
    fill_rows(second_flat, 1)
    start_rows(1)
    fill_columns(packed, 1, 1)
    start_columns(1, 1)

    flat = final.reshape(planes * rows, 128)

    def take(part):
        half = rows // 8

        def four_rows(i, carry):
            start = 4 * (half // 2 + i) if part == 0 else 4 * jnp.where(i < half // 2, i, i + half)
            for j in range(4):
                value = flat[pl.ds(start + j, planes, stride=rows), :]
                high = value.astype(jnp.bfloat16)
                rest = (value - high.astype(jnp.float32)).astype(jnp.bfloat16)
                halves[pl.ds(0, planes), pl.ds(j * 128, 128)] = high
                halves[pl.ds(planes, planes), pl.ds(j * 128, 128)] = rest
            chosen = pick[pl.ds(pl.multiple_of(start * 128, 512), 512), :]
            taken[...] += jnp.dot(halves[...], chosen, preferred_element_type=jnp.float32)
            return carry

        lax.fori_loop(0, half, four_rows, 0)

    wait_columns(1, 0)
    place_columns(1, 0)
    second_step(0)
    take(0)
    wait_rows(1)
    place_rows(second_flat, 1)
    wait_columns(1, 1)
    place_columns(1, 1)
    second_step(1)
    take(1)
    outbox[...] = jnp.transpose(taken[pl.ds(0, planes), :] + taken[pl.ds(planes, planes), :]) + tally

    own = pl.ds(pl.multiple_of(me * BOX, BOX), BOX)

    def box_start(j, carry):
        other = after_me(j)
        pltpu.make_async_remote_copy(
            src_ref=outbox.at[pl.ds(pl.multiple_of(other * BOX, BOX), CAP + 1)],
            dst_ref=inbox.at[pl.ds(pl.multiple_of(me * BOX, BOX), CAP + 1)],
            send_sem=box_send.at[0],
            recv_sem=box_recv.at[0],
            device_id=(lax.div(other, n_lon), lax.rem(other, n_lon)),
            device_id_type=MESH,
        ).start()
        return carry

    lax.fori_loop(1, n_dev, box_start, 0)
    others = pl.ds(0, (n_dev - 1) * (CAP + 1))
    pltpu.make_async_remote_copy(
        src_ref=outbox.at[others],
        dst_ref=inbox.at[others],
        send_sem=box_send.at[0],
        recv_sem=box_recv.at[0],
        device_id=(lat, right),
        device_id_type=MESH,
    ).wait()
    inbox[own, :] = outbox[own, :]
    for i in range(CAP):
        arrivals[pl.ds(i, n_dev, stride=CAP), :] = inbox[pl.ds(i, n_dev, stride=BOX), :]
    told = inbox[pl.ds(CAP, n_dev, stride=BOX), :][:, :n_dev]
    straight = lax.broadcasted_iota(jnp.int32, (n_dev, n_dev), 0) == lax.broadcasted_iota(
        jnp.int32, (n_dev, n_dev), 1
    )
    counts[...] = jnp.sum(jnp.where(straight, told, 0.0), axis=0, keepdims=True).astype(jnp.int32)


def local(tracers, vel_east, vel_north, land_mask, step_area, float_cell, float_owner):
    tracer_count, levels, rows, columns = tracers.shape
    n_lat, n_lon = lax.axis_size("lat"), lax.axis_size("lon")
    n_dev = n_lat * n_lon
    planes = tracer_count * levels
    tall = rows + 2 * PADR
    floats = float_cell.shape[0]
    row_size = 2 * planes + levels
    col_size = (tracer_count // 2 + 1) * max(rows - 16, 16)
    f32 = jnp.float32
    whole = pl.BlockSpec(memory_space=pl.ANY)
    vmem = pl.BlockSpec(memory_space=pltpu.VMEM)
    out, arrivals, counts = pl.pallas_call(
        functools.partial(kernel, (tracer_count, levels, rows, n_lat, n_lon)),
        out_shape=(
            pltpu.VMEM((planes, rows, columns), f32),
            pltpu.VMEM((n_dev * CAP, planes), f32),
            pltpu.VMEM((1, n_dev), jnp.int32),
        ),
        in_specs=[whole] * 7,
        out_specs=[vmem] * 3,
        scratch_shapes=[
            pltpu.VMEM((rows, columns), f32),
            pltpu.VMEM((1, floats), jnp.int32),
            pltpu.VMEM((1, floats), jnp.int32),
            pltpu.VMEM((levels, rows, columns), jnp.int32),
            pltpu.VMEM((levels, rows, columns), f32),
            pltpu.VMEM((levels, rows, columns), f32),
            pltpu.VMEM((planes, tall, columns), f32),
            pltpu.VMEM((planes, tall, columns), f32),
            pltpu.VMEM((levels, tall, columns), f32),
            pltpu.VMEM((levels, tall, columns), f32),
            pltpu.VMEM((levels, 9, rows, columns), f32),
            pltpu.VMEM((tracer_count + 1, rows, columns), f32),
            *[pltpu.VMEM((2, 2, col_size, columns), f32)] * 4,
            *[pltpu.VMEM((2, row_size, columns), f32)] * 4,
            pltpu.VMEM((rows * columns, n_dev * BOX), jnp.bfloat16),
            pltpu.VMEM((2 * planes, 4 * columns), jnp.bfloat16),
            pltpu.VMEM((2 * planes, n_dev * BOX), f32),
            pltpu.VMEM((n_dev * BOX, planes), f32),
            pltpu.VMEM((n_dev * BOX, planes), f32),
            pltpu.SemaphoreType.DMA((7,)),
            pltpu.SemaphoreType.DMA((2, 6)),
            pltpu.SemaphoreType.DMA((2, 6)),
            pltpu.SemaphoreType.DMA((1,)),
            pltpu.SemaphoreType.DMA((1,)),
        ],
        compiler_params=pltpu.CompilerParams(
            collective_id=0, has_side_effects=True, vmem_limit_bytes=56 * 1024 * 1024
        ),
        cost_estimate=pl.CostEstimate(
            flops=2 * 17 * planes * rows * columns, bytes_accessed=8 * 1024 * 1024, transcendentals=0
        ),
    )(
        step_area,
        float_cell.reshape(1, floats),
        float_owner.reshape(1, floats),
        land_mask,
        vel_east,
        vel_north,
        tracers.reshape(planes, rows, columns),
    )
    return out.reshape(tracers.shape), arrivals, counts.reshape(n_dev)


def solution(mesh):
    placed = (
        P(None, None, "lat", "lon"),
        P(None, "lat", "lon"),
        P(None, "lat", "lon"),
        P(None, "lat", "lon"),
        P("lat", "lon"),
        P(("lat", "lon")),
        P(("lat", "lon"), None),
    )
    return jax.shard_map(
        local,
        mesh=mesh,
        in_specs=placed,
        out_specs=(P(None, None, "lat", "lon"), P(("lat", "lon"), None), P(("lat", "lon"))),
        check_vma=False,
    )
```
